32 devices in a mesh: seq: 4 (over x, core), dp: 8 (over z, y).
Axes of the slice: x: 2, y: 2, z: 4, core: 2. Of those that a mesh axis runs over, the one named last changes fastest.
Arguments:
- characters: bfloat16 [16, 2048, 768], P('dp', 'seq'), may hold values from -6 to 6
- cotangent: bfloat16 [16, 2048, 768], P('dp', 'seq'), may hold values from -6 to 6
- lengths: int32 [16], P('dp'), may hold values from 200 to 2048, as said below
- vectors: float32 [12, 768], replicated, may hold values from -0.6 to 1.4
- vector_acc: float32 [12, 768], replicated, may hold values from 1 to 4
- attend_weight: float32 [768, 4, 768], P(None, None, ('seq', 'dp')), may hold values from -1.7320508 to 1.7320508
- attend_moment: float32 [768, 4, 768], P(None, None, ('seq', 'dp')), may hold values from -4 to 4
- attend_left: float32 [768, 4, 768], P(('seq', 'dp')), may hold values from 0 to 4, as said below
- attend_right: float32 [768, 4, 768], P(None, None, ('seq', 'dp')), may hold values from 0 to 4, as said below
- attend_rootleft: float32 [768, 4, 768], P(('seq', 'dp')), may hold values from -0.1 to 1.7
- attend_rootright: float32 [768, 4, 768], P(None, None, ('seq', 'dp')), may hold values from -0.1 to 1.7
- expand_weight: float32 [768, 3072], P(None, ('seq', 'dp')), may hold values from -0.21875 to 0.21875
- expand_moment: float32 [768, 3072], P(None, ('seq', 'dp')), may hold values from -4 to 4
- expand_left: float32 [768, 768], P(('seq', 'dp')), may hold values from 0 to 4, as said below
- expand_right: float32 [3072, 3072], P(None, ('seq', 'dp')), may hold values from 0 to 4, as said below
- expand_rootleft: float32 [768, 768], P(('seq', 'dp')), may hold values from -0.1 to 1.7
- expand_rootright: float32 [3072, 3072], P(None, ('seq', 'dp')), may hold values from -0.1 to 1.7
- shrink_weight: float32 [3072, 768], P(None, ('seq', 'dp')), may hold values from -0.109375 to 0.109375
- shrink_moment: float32 [3072, 768], P(None, ('seq', 'dp')), may hold values from -4 to 4
- shrink_left: float32 [3072, 3072], P(('seq', 'dp')), may hold values from 0 to 4, as said below
- shrink_right: float32 [768, 768], P(None, ('seq', 'dp')), may hold values from 0 to 4, as said below
- shrink_rootleft: float32 [3072, 3072], P(('seq', 'dp')), may hold values from -0.1 to 1.7
- shrink_rootright: float32 [768, 768], P(None, ('seq', 'dp')), may hold values from -0.1 to 1.7
Outputs:
- layer_output: bfloat16 [16, 2048, 768], P('dp', 'seq')
- characters_grad: bfloat16 [16, 2048, 768], P('dp', 'seq')
- attend_grad: float32 [768, 4, 768], P(('seq', 'dp'))
- attend_newmoment: float32 [768, 4, 768], P(None, None, ('seq', 'dp'))
- attend_newweight: float32 [768, 4, 768], P(None, None, ('seq', 'dp'))
- attend_newleft: float32 [768, 4, 768], P(('seq', 'dp'))
- attend_newright: float32 [768, 4, 768], P(None, None, ('seq', 'dp'))
- expand_grad: float32 [768, 3072], P(('seq', 'dp'))
- expand_newmoment: float32 [768, 3072], P(None, ('seq', 'dp'))
- expand_newweight: float32 [768, 3072], P(None, ('seq', 'dp'))
- expand_newleft: float32 [768, 768], P(('seq', 'dp'))
- expand_newright: float32 [3072, 3072], P(None, ('seq', 'dp'))
- shrink_grad: float32 [3072, 768], P(('seq', 'dp'))
- shrink_newmoment: float32 [3072, 768], P(None, ('seq', 'dp'))
- shrink_newweight: float32 [3072, 768], P(None, ('seq', 'dp'))
- shrink_newleft: float32 [3072, 3072], P(('seq', 'dp'))
- shrink_newright: float32 [768, 768], P(None, ('seq', 'dp'))
- vector_grad: float32 [12, 768], replicated
- vector_newacc: float32 [12, 768], replicated
- vector_new: float32 [12, 768], replicated
The draws below stay inside these ranges and needn't reach their ends.
Inputs may be any that keep to these rules, and one draw needn't show every extreme that they name: `lengths`: among the texts of each index of dp (runs of 2), one text chosen by the seed has length 2048. `attend_left`: Symmetric. `attend_right`: Symmetric. `expand_left`: Symmetric. `expand_right`: Symmetric. `shrink_left`: Symmetric. `shrink_right`: Symmetric.
All inputs are finite; a program needn't handle non-finite values.
Results may differ from the reference program's by a relative error of at most 0.0099.
Values may be sent and summed in bfloat16 or wider, within the bound.
No kernel may reach another device: no remote copies, remote signals or barrier semaphores. Data moves between devices by JAX's collectives and lax.ppermute only.
A program may use at most 256 MiB of HBM per device.

```python
import math
import jax
import jax.numpy as jnp
from jax import lax

D = 768
HEADS = 12
HEAD = 64
FF = 3072
WIN = 128
TXT_DEV = 2
TEXTS = 16
SEQ = 2048
TOKENS = 32768
MINLEN = 200
VROWS = 12


def diagonal_stat(key, extent, slot_count, low_end, high_end):
    diagonal_values = jnp.exp(jax.random.uniform(key, (extent, slot_count, 1), jnp.float32, math.log(low_end), math.log(high_end)))
    identity = (jnp.arange(extent)[:, None, None] == jnp.arange(extent)[None, None, :]).astype(jnp.float32)
    return identity * diagonal_values


def root_stat(key, extent, slot_count):
    diagonal_key, other_key = jax.random.split(key)
    base_matrix = diagonal_stat(diagonal_key, extent, slot_count, 0.6, 1.6)
    noise_part = jax.random.uniform(other_key, (extent, slot_count, extent), jnp.float32, -1.0, 1.0)
    symmetric = (noise_part + jnp.transpose(noise_part, (2, 1, 0))) * (0.6 / math.sqrt(extent))
    return base_matrix + symmetric


def draw_lengths(key, part):
    key = jax.random.fold_in(key, 11)
    base_key, pick_key = jax.random.split(key)
    base_lengths = jax.random.randint(base_key, (TEXTS,), MINLEN, SEQ + 1)
    chosen = jax.random.randint(pick_key, (TEXTS // TXT_DEV,), 0, TXT_DEV)
    order = jnp.arange(TEXTS)
    longest = order % TXT_DEV == jnp.repeat(chosen, TXT_DEV)
    return jnp.where(longest, SEQ, base_lengths).astype(jnp.int32)


def draw_vectors(key, part):
    key = jax.random.fold_in(key, 12)
    first_key, second_key = jax.random.split(key)
    row_index = jnp.arange(VROWS)[:, None]
    biases = jax.random.uniform(first_key, (VROWS, D), jnp.float32, -0.6, 0.6)
    gain_rows = 1.0 + jax.random.uniform(second_key, (VROWS, D), jnp.float32, -0.4, 0.4)
    return jnp.where((row_index == 0) | (row_index == 5), gain_rows, biases)


def draw_attend_weight(key, part):
    key = jax.random.fold_in(key, 20)
    slot_index = jnp.arange(4)[None, :, None]
    spread = jnp.where(slot_index == 3, math.sqrt(2.0 * WIN / D), 1.0 / math.sqrt(D))
    return jax.random.truncated_normal(key, -3.0, 3.0, (D, 4, D), jnp.float32) * spread


def draw_attend_left(key, part):
    key = jax.random.fold_in(key, 21)
    return diagonal_stat(key, D, 4, 1.0, 4.0)


def draw_attend_right(key, part):
    key = jax.random.fold_in(key, 22)
    return diagonal_stat(key, D, 4, 1.0, 4.0)


def draw_attend_rootleft(key, part):
    key = jax.random.fold_in(key, 23)
    return root_stat(key, D, 4)


def draw_attend_rootright(key, part):
    key = jax.random.fold_in(key, 24)
    return root_stat(key, D, 4)


def draw_expand_left(key, part):
    key = jax.random.fold_in(key, 31)
    return diagonal_stat(key, D, 1, 1.0, 4.0)[:, 0, :]


def draw_expand_right(key, part):
    key = jax.random.fold_in(key, 32)
    return diagonal_stat(key, FF, 1, 1.0, 4.0)[:, 0, :]


def draw_expand_rootleft(key, part):
    key = jax.random.fold_in(key, 33)
    return root_stat(key, D, 1)[:, 0, :]


def draw_expand_rootright(key, part):
    key = jax.random.fold_in(key, 34)
    return root_stat(key, FF, 1)[:, 0, :]


def draw_shrink_left(key, part):
    key = jax.random.fold_in(key, 41)
    return diagonal_stat(key, FF, 1, 1.0, 4.0)[:, 0, :]


def draw_shrink_right(key, part):
    key = jax.random.fold_in(key, 42)
    return diagonal_stat(key, D, 1, 1.0, 4.0)[:, 0, :]


def draw_shrink_rootleft(key, part):
    key = jax.random.fold_in(key, 43)
    return root_stat(key, FF, 1)[:, 0, :]


def draw_shrink_rootright(key, part):
    key = jax.random.fold_in(key, 44)
    return root_stat(key, D, 1)[:, 0, :]


def block_levels(own_key, shape, cuts, low, high):
    factor_of, own = 1.0, jax.random.fold_in(own_key, 6)
    for dim, shards_of in cuts:
        draws = jnp.exp(jax.random.uniform(jax.random.fold_in(own, dim), (shards_of,), jnp.float32, low / len(cuts), high / len(cuts)))
        factor_of = factor_of * jnp.repeat(draws, shape[dim] // shards_of).reshape([-1 if axis == dim else 1 for axis in range(len(shape))])
    return factor_of


def gaussian(stream_key, shape, scale, reach, cuts=(), kind=jnp.bfloat16):
    result = jax.random.normal(stream_key, shape, jnp.float32) * scale
    if len(cuts) > 0:
        result = block_levels(stream_key, shape, cuts, -0.22, 0.18) * result
    return jnp.clip(result, min=-reach, max=reach).astype(kind)


def setup_inputs(seed: int = 0) -> dict:
    seeds = jax.random.split(jax.random.key(seed), 24)
    characters = gaussian(seeds[0], (TEXTS, SEQ, D), 1.0, 6.0, ((0, 8), (1, 4)))
    cotangent = gaussian(seeds[1], (TEXTS, SEQ, D), 1.0, 6.0, ((0, 8), (1, 4)))
    lengths = draw_lengths(jax.random.fold_in(seeds[23], 71), 0)
    vectors = draw_vectors(jax.random.fold_in(seeds[23], 71), 0)
    vector_acc = jnp.clip(jnp.exp(jax.random.uniform(seeds[4], (VROWS, D), jnp.float32, math.log(1.0), math.log(4.0))), 1.0, 4.0)
    attend_weight = draw_attend_weight(jax.random.fold_in(seeds[23], 71), 0)
    attend_moment = gaussian(seeds[6], (D, 4, D), 1.0, 4.0, ((2, 32),), jnp.float32)
    attend_left = draw_attend_left(jax.random.fold_in(seeds[23], 71), 0)
    attend_right = draw_attend_right(jax.random.fold_in(seeds[23], 71), 0)
    attend_rootleft = draw_attend_rootleft(jax.random.fold_in(seeds[23], 71), 0)
    attend_rootright = draw_attend_rootright(jax.random.fold_in(seeds[23], 71), 0)
    expand_weight = gaussian(seeds[11], (D, FF), D ** -0.5, 0.21875, ((1, 32),), jnp.float32)
    expand_moment = gaussian(seeds[12], (D, FF), 1.0, 4.0, ((1, 32),), jnp.float32)
    expand_left = draw_expand_left(jax.random.fold_in(seeds[23], 71), 0)
    expand_right = draw_expand_right(jax.random.fold_in(seeds[23], 71), 0)
    expand_rootleft = draw_expand_rootleft(jax.random.fold_in(seeds[23], 71), 0)
    expand_rootright = draw_expand_rootright(jax.random.fold_in(seeds[23], 71), 0)
    shrink_weight = gaussian(seeds[17], (FF, D), FF ** -0.5, 0.109375, ((1, 32),), jnp.float32)
    shrink_moment = gaussian(seeds[18], (FF, D), 1.0, 4.0, ((1, 32),), jnp.float32)
    shrink_left = draw_shrink_left(jax.random.fold_in(seeds[23], 71), 0)
    shrink_right = draw_shrink_right(jax.random.fold_in(seeds[23], 71), 0)
    shrink_rootleft = draw_shrink_rootleft(jax.random.fold_in(seeds[23], 71), 0)
    shrink_rootright = draw_shrink_rootright(jax.random.fold_in(seeds[23], 71), 0)
    return dict(characters=characters, cotangent=cotangent, lengths=lengths, vectors=vectors, vector_acc=vector_acc, attend_weight=attend_weight, attend_moment=attend_moment, attend_left=attend_left, attend_right=attend_right, attend_rootleft=attend_rootleft, attend_rootright=attend_rootright, expand_weight=expand_weight, expand_moment=expand_moment, expand_left=expand_left, expand_right=expand_right, expand_rootleft=expand_rootleft, expand_rootright=expand_rootright, shrink_weight=shrink_weight, shrink_moment=shrink_moment, shrink_left=shrink_left, shrink_right=shrink_right, shrink_rootleft=shrink_rootleft, shrink_rootright=shrink_rootright)


EPSILON = 1e-05
STAT_EPSILON = 1e-06
MATRIX_RATE = 0.5
VECTOR_RATE = 0.3
MOMENTUM = 0.9
MASKED = -1e+30
HIGHEST = lax.Precision.HIGHEST

@jax.custom_vjp
def low(v):
    return lax.optimization_barrier(v.astype(jnp.bfloat16)).astype(jnp.float32)

@jax.custom_vjp
def low_back(v):
    return v

def low_keep(v):
    return (low(v), None)

def low_pass(kept, grad):
    return (grad,)

def back_keep(v):
    return (v, None)

def back_low(kept, grad):
    return (low(grad),)
low.defvjp(low_keep, low_pass)
low_back.defvjp(back_keep, back_low)

def normalize(values, gain_row, bias_row):
    centre = values - lax.optimization_barrier(jnp.mean(values, axis=-1, keepdims=True))
    spread = lax.optimization_barrier(jnp.mean(centre * centre, axis=-1, keepdims=True))
    return centre * lax.rsqrt(spread + EPSILON) * gain_row + bias_row

def matmul(left_side, right_side):
    return jnp.dot(left_side, right_side, precision=HIGHEST, preferred_element_type=jnp.float32)

def text_layer(inputs, length, vectors, query_w, key_w, value_w, out_w, expand_low, shrink_low):
    normed = low(normalize(inputs, vectors[0], vectors[1]))
    queries = low(low_back(matmul(normed, query_w) + vectors[2])).reshape(SEQ, HEADS, HEAD)
    keys_low = low(low_back(matmul(normed, key_w))).reshape(SEQ, HEADS, HEAD)
    values_low = low(low_back(matmul(normed, value_w) + vectors[3])).reshape(SEQ, HEADS, HEAD)
    scores = low_back(jnp.einsum('qhe,khe->hqk', queries, keys_low, precision=HIGHEST) * 0.125)
    positions = jnp.arange(SEQ, dtype=jnp.int32)
    near = jnp.abs(positions[:, None] - positions[None, :]) <= WIN
    allowed = near & ((positions[None, :] < length) | (positions[:, None] == positions[None, :]))
    scores = jnp.where(allowed[None], scores, MASKED)
    attention = low(jax.nn.softmax(scores, axis=-1))
    attended = jnp.einsum('hqk,khe->qhe', attention, values_low, precision=HIGHEST).reshape(SEQ, D)
    attended = low(low_back(attended))
    branch = low_back(matmul(attended, out_w) + vectors[4])
    middle = inputs + branch
    normed_two = low(normalize(middle, vectors[5], vectors[6]))
    expanded = low_back(matmul(normed_two, expand_low) + vectors[8:].reshape(FF))
    gated_low = low(jax.nn.gelu(expanded, approximate=False))
    return middle + low_back(matmul(gated_low, shrink_low) + vectors[7])

def forward(inputs, vectors, attend_w, expand_w, shrink_w, lengths):
    query_w = low(attend_w[:, 0, :])
    key_w = low(attend_w[:, 1, :])
    value_w = low(attend_w[:, 2, :])
    out_w = low(attend_w[:, 3, :])
    expand_low = low(expand_w)
    shrink_low = low(shrink_w)

    def per_text(packed):
        return text_layer(packed[0], packed[1], vectors, query_w, key_w, value_w, out_w, expand_low, shrink_low)
    return lax.map(jax.checkpoint(per_text), (inputs, lengths))

def shampoo(grad_raw, weight, moment, left, right, rootleft, rootright):
    scaled = grad_raw / math.sqrt(TOKENS)
    row_count = scaled.shape[0]
    col_count = scaled.shape[2]
    mean_square = lax.optimization_barrier(jnp.mean(scaled * scaled, axis=(0, 2), keepdims=True)) + STAT_EPSILON
    new_left = 0.5 * left + 0.5 * jnp.einsum('rwk,iwk->rwi', scaled, scaled, precision=HIGHEST) / (col_count * mean_square)
    new_right = 0.5 * right + 0.5 * jnp.einsum('iwk,iwj->kwj', scaled, scaled, precision=HIGHEST) / (row_count * mean_square)
    left_applied = jnp.einsum('rwi,iwj->rwj', rootleft, scaled, precision=HIGHEST)
    direction = jnp.einsum('iwk,kwj->iwj', left_applied, rootright, precision=HIGHEST)
    new_moment = MOMENTUM * moment + direction * lax.rsqrt(mean_square)
    new_weight = weight - MATRIX_RATE / math.sqrt(row_count) * new_moment
    return (scaled, new_moment, new_weight, new_left, new_right)

def flat(triple_array):
    return triple_array[:, 0, :]

def reference(characters, cotangent, lengths, vectors, vector_acc, attend_weight, attend_moment, attend_left, attend_right, attend_rootleft, attend_rootright, expand_weight, expand_moment, expand_left, expand_right, expand_rootleft, expand_rootright, shrink_weight, shrink_moment, shrink_left, shrink_right, shrink_rootleft, shrink_rootright):
    inputs = characters.astype(jnp.float32)

    def wrapped(inputs_in, vectors_in, attend_in, expand_in, shrink_in):
        return forward(inputs_in, vectors_in, attend_in, expand_in, shrink_in, lengths)
    output, pullback = jax.vjp(wrapped, inputs, vectors, attend_weight, expand_weight, shrink_weight)
    input_grad, vector_raw, attend_raw, expand_raw, shrink_raw = pullback(cotangent.astype(jnp.float32))
    attend_out = shampoo(attend_raw, attend_weight, attend_moment, attend_left, attend_right, attend_rootleft, attend_rootright)
    expand_out = shampoo(expand_raw[:, None, :], expand_weight[:, None, :], expand_moment[:, None, :], expand_left[:, None, :], expand_right[:, None, :], expand_rootleft[:, None, :], expand_rootright[:, None, :])
    shrink_out = shampoo(shrink_raw[:, None, :], shrink_weight[:, None, :], shrink_moment[:, None, :], shrink_left[:, None, :], shrink_right[:, None, :], shrink_rootleft[:, None, :], shrink_rootright[:, None, :])
    vector_grad = vector_raw / math.sqrt(TOKENS)
    vector_newacc = vector_acc + vector_grad * vector_grad
    vector_new = vectors - VECTOR_RATE * vector_grad / (jnp.sqrt(vector_newacc) + 1e-08)
    return (output.astype(jnp.bfloat16), input_grad.astype(jnp.bfloat16), attend_out[0], attend_out[1], attend_out[2], attend_out[3], attend_out[4], flat(expand_out[0]), flat(expand_out[1]), flat(expand_out[2]), flat(expand_out[3]), flat(expand_out[4]), flat(shrink_out[0]), flat(shrink_out[1]), flat(shrink_out[2]), flat(shrink_out[3]), flat(shrink_out[4]), vector_grad, vector_newacc, vector_new)
```

```python
import functools
import math

import jax
import jax.numpy as jnp
from jax import lax
from jax.experimental import pallas as pl
from jax.experimental.pallas import tpu as pltpu
from jax.sharding import PartitionSpec as P

HEAD = 64
WIN = 128
PAIR = 2 * HEAD
KEYS = 3 * WIN
VMEM_BYTES = 56 * 1024 * 1024

EPSILON = 1e-05
STAT_EPSILON = 1e-06
MATRIX_RATE = 0.5
VECTOR_RATE = 0.3
MOMENTUM = 0.9
MASKED = -1e30

TAIL_SLOPE = 0.372
TAIL_POLY = (
    0.14840650094319077,
    0.14841262582366468,
    0.1276493296855659,
    0.0898105241362328,
    0.013338554384341726,
    0.06117535709592349,
    -0.19401880881817585,
    0.1376568075417028,
    -0.0324309766125075,
)


def nt(left_rows, right_rows):
    return lax.dot_general(
        left_rows, right_rows, (((1,), (1,)), ((), ())), preferred_element_type=jnp.float32
    )


def nn(left_rows, right_cols):
    return jnp.dot(left_rows, right_cols, preferred_element_type=jnp.float32)


def across(left_rows, right_rows):
    return lax.dot_general(
        left_rows, right_rows, (((0,), (0,)), ((), ())), preferred_element_type=jnp.float32
    )


def low(values):
    return values.astype(jnp.bfloat16)


def normalize(values, gain_row, bias_row):
    centre = values - jnp.mean(values, axis=-1, keepdims=True)
    spread = jnp.mean(centre * centre, axis=-1, keepdims=True)
    return centre * lax.rsqrt(spread + EPSILON) * gain_row + bias_row


def params():
    return pltpu.CompilerParams(vmem_limit_bytes=VMEM_BYTES)


def write_mask(bias_ref, length, base, blocks):
    for i in range(blocks):
        key = lax.broadcasted_iota(jnp.int32, (KEYS, WIN), 0)
        query = lax.broadcasted_iota(jnp.int32, (KEYS, WIN), 1)
        place = key + (base + (i - 1) * WIN)
        near = (key >= query) & (key <= query + 2 * WIN)
        seen = ((place >= 0) & (place < length)) | (key == query + WIN)
        bias_ref[i] = jnp.where(near & seen, 0.0, MASKED)


def stacked(rows, scale):
    lane = lax.broadcasted_iota(jnp.int32, rows.shape, 1)
    rows = rows.astype(jnp.float32) * scale
    first = jnp.where(lane < HEAD, rows, 0.0)
    second = jnp.where(lane < HEAD, 0.0, rows)
    return low(jnp.concatenate([first, second], axis=0))


def unstacked(turned):
    pair = jnp.concatenate([turned[:HEAD, :WIN], turned[HEAD:, WIN:]], axis=0)
    return pair.T


def attend_forward(blocks, lengths, base, q_ref, k_ref, v_ref, o_ref, total_ref, bias_ref):
    text = pl.program_id(0)

    @pl.when(pl.program_id(1) == 0)
    def _():
        write_mask(bias_ref, lengths[text], base[0], blocks)

    for i in range(blocks):
        keys = k_ref[0, i * WIN : i * WIN + KEYS, :]
        values = v_ref[0, i * WIN : i * WIN + KEYS, :]
        queries = stacked(q_ref[0, i * WIN : (i + 1) * WIN, :], 0.125)
        bias = bias_ref[i]
        scores = nt(keys, queries) + jnp.concatenate([bias, bias], axis=1)
        peak = jnp.max(scores, axis=0, keepdims=True)
        weights = jnp.exp(scores - peak)
        total = jnp.sum(weights, axis=0, keepdims=True)
        mixed = across(values, low(weights)) * (1.0 / total)
        o_ref[0, i * WIN : (i + 1) * WIN, :] = low(unstacked(mixed))
        log_total = peak + jnp.log(total)
        total_ref[0, 0, 2 * i : 2 * i + 1, :] = log_total[:, :WIN]
        total_ref[0, 0, 2 * i + 1 : 2 * i + 2, :] = log_total[:, WIN:]


def attend_backward(
    blocks,
    lengths,
    base,
    q_ref,
    k_ref,
    v_ref,
    up_ref,
    total_ref,
    dq_ref,
    dk_ref,
    dv_ref,
    bias_ref,
    dk_sum,
    dv_sum,
):
    text = pl.program_id(0)

    @pl.when(pl.program_id(1) == 0)
    def _():
        write_mask(bias_ref, lengths[text], base[0], blocks)

    dk_sum[...] = jnp.zeros_like(dk_sum)
    dv_sum[...] = jnp.zeros_like(dv_sum)
    for i in range(blocks):
        window = slice(i * WIN, i * WIN + KEYS)
        own = slice(i * WIN, (i + 1) * WIN)
        keys = k_ref[0, window, :]
        values = v_ref[0, window, :]
        queries = stacked(q_ref[0, own, :], 0.125)
        upstream = stacked(up_ref[0, own, :], 1.0)
        bias = bias_ref[i]
        log_total = jnp.concatenate(
            [total_ref[0, 0, 2 * i : 2 * i + 1, :], total_ref[0, 0, 2 * i + 1 : 2 * i + 2, :]],
            axis=1,
        )
        scores = nt(keys, queries) + jnp.concatenate([bias, bias], axis=1)
        weights = jnp.exp(scores - log_total)
        weight_grad = nt(values, upstream)
        product = weights * weight_grad
        score_grad = low(product - weights * jnp.sum(product, axis=0, keepdims=True))
        dv_sum[window, :] += nn(low(weights), upstream)
        dk_sum[window, :] += nn(score_grad, queries)
        dq_ref[0, own, :] = low(unstacked(across(keys, score_grad)) * 0.125)
    dk_ref[0] = low(dk_sum[...])
    dv_ref[0] = low(dv_sum[...])


def attention_specs(block_size):
    wide = block_size + 2 * WIN
    blocks = block_size // WIN
    own = pl.BlockSpec((1, block_size, PAIR), lambda t, g: (t, 0, g))
    ext = pl.BlockSpec((1, wide, PAIR), lambda t, g: (t, 0, g))
    sums = pl.BlockSpec((1, 1, 2 * blocks, WIN), lambda t, g: (t, g, 0, 0))
    smem = pl.BlockSpec(memory_space=pltpu.SMEM)
    return wide, blocks, own, ext, sums, smem


def run_forward(lengths, base, query, key_ext, value_ext):
    texts, block_size, width = query.shape
    wide, blocks, own, ext, sums, smem = attention_specs(block_size)
    work = texts * blocks * (width // PAIR)
    return pl.pallas_call(
        functools.partial(attend_forward, blocks),
        grid=(texts, width // PAIR),
        in_specs=[smem, smem, own, ext, ext],
        out_specs=[own, sums],
        out_shape=[
            jax.ShapeDtypeStruct(query.shape, jnp.bfloat16),
            jax.ShapeDtypeStruct((texts, width // PAIR, 2 * blocks, WIN), jnp.float32),
        ],
        scratch_shapes=[pltpu.VMEM((blocks, KEYS, WIN), jnp.float32)],
        compiler_params=params(),
        cost_estimate=pl.CostEstimate(
            flops=work * 4 * KEYS * PAIR * 2 * WIN,
            bytes_accessed=query.size * 2 * 5,
            transcendentals=work * KEYS * 2 * WIN,
        ),
        name="attend_forward",
    )(lengths, base, query, key_ext, value_ext)


def run_backward(lengths, base, query, key_ext, value_ext, upstream, totals):
    texts, block_size, width = query.shape
    wide, blocks, own, ext, sums, smem = attention_specs(block_size)
    work = texts * blocks * (width // PAIR)
    return pl.pallas_call(
        functools.partial(attend_backward, blocks),
        grid=(texts, width // PAIR),
        in_specs=[smem, smem, own, ext, ext, own, sums],
        out_specs=[own, ext, ext],
        out_shape=[
            jax.ShapeDtypeStruct(query.shape, jnp.bfloat16),
            jax.ShapeDtypeStruct(key_ext.shape, jnp.bfloat16),
            jax.ShapeDtypeStruct(key_ext.shape, jnp.bfloat16),
        ],
        scratch_shapes=[
            pltpu.VMEM((blocks, KEYS, WIN), jnp.float32),
            pltpu.VMEM((wide, PAIR), jnp.float32),
            pltpu.VMEM((wide, PAIR), jnp.float32),
        ],
        compiler_params=params(),
        cost_estimate=pl.CostEstimate(
            flops=work * 10 * KEYS * PAIR * 2 * WIN,
            bytes_accessed=query.size * 2 * 10,
            transcendentals=work * KEYS * 2 * WIN,
        ),
        name="attend_backward",
    )(lengths, base, query, key_ext, value_ext, upstream, totals)


GATE_ROWS = 256
GATE_SLAB = 16


def gate_kernel(rows_ref, weight_ref, bias_ref, gate_ref, slope_ref, hidden):
    hidden[...] = nt(rows_ref[...], weight_ref[...])

    def slab(i, carry):
        own = pl.ds(pl.multiple_of(i * GATE_SLAB, GATE_SLAB), GATE_SLAB)
        u = hidden[own, :] + bias_ref[...]
        bell = jnp.exp(-0.5 * (u * u))
        t = 1.0 / (1.0 + TAIL_SLOPE * jnp.abs(u))
        poly = TAIL_POLY[-1] * t + TAIL_POLY[-2]
        for term in TAIL_POLY[-3::-1]:
            poly = poly * t + term
        tail = poly * t * bell
        phi = jnp.where(u < 0.0, tail, 1.0 - tail)
        gate_ref[own, :] = low(u * phi)
        slope_ref[own, :] = low(phi + u * bell * (1.0 / math.sqrt(2.0 * math.pi)))
        return carry

    lax.fori_loop(0, GATE_ROWS // GATE_SLAB, slab, 0, unroll=2)


def run_gate(rows, weight_t, bias):
    tokens, width = rows.shape
    hidden = weight_t.shape[0]
    part = width
    out = jax.ShapeDtypeStruct((tokens, hidden), jnp.bfloat16)
    return pl.pallas_call(
        gate_kernel,
        grid=(hidden // part, tokens // GATE_ROWS),
        in_specs=[
            pl.BlockSpec((GATE_ROWS, width), lambda j, i: (i, 0)),
            pl.BlockSpec((part, width), lambda j, i: (j, 0)),
            pl.BlockSpec((1, part), lambda j, i: (0, j)),
        ],
        out_specs=[pl.BlockSpec((GATE_ROWS, part), lambda j, i: (i, j))] * 2,
        out_shape=[out, out],
        scratch_shapes=[pltpu.VMEM((GATE_ROWS, part), jnp.float32)],
        compiler_params=params(),
        cost_estimate=pl.CostEstimate(
            flops=2 * tokens * width * hidden,
            bytes_accessed=2 * (tokens * width + width * hidden + 2 * tokens * hidden),
            transcendentals=2 * tokens * hidden,
        ),
        name="gate",
    )(rows, weight_t, bias)


def core_swap(blocks):
    count = lax.axis_size("seq")
    return lax.ppermute(blocks, "seq", [(i, i ^ 1) for i in range(count)])


def chip_swap(blocks):
    count = lax.axis_size("seq")
    return lax.ppermute(blocks, "seq", [(i, i ^ 2) for i in range(count)])


def swap(blocks):
    return lax.all_to_all(blocks, "seq", split_axis=0, concat_axis=0, tiled=True)


def spread(block):
    count = lax.axis_size("dp")
    copies = jnp.broadcast_to(block[None], (count,) + block.shape)
    return lax.all_to_all(copies, "dp", split_axis=0, concat_axis=0, tiled=True)


def ordered(index, own, other):
    return jnp.where(index == 0, jnp.stack([own, other]), jnp.stack([other, own]))


def add_low(left, right):
    return low(left.astype(jnp.float32) + right.astype(jnp.float32))


def summed(matrices, core, chip, blocks_of):
    first, second, third, fourth = matrices
    lower = jnp.stack([first, third])
    upper = jnp.stack([second, fourth])
    sent = jnp.where(core == 0, upper, lower)
    kept = jnp.where(core == 0, lower, upper)
    both = add_low(kept, core_swap(sent))
    sent = jnp.where(chip == 0, both[1], both[0])
    kept = jnp.where(chip == 0, both[0], both[1])
    one = add_low(kept, chip_swap(sent))
    got = lax.all_to_all(blocks_of(one), "dp", split_axis=0, concat_axis=0, tiled=True)
    return jnp.sum(got.astype(jnp.float32), axis=0)


def thirds(value):
    high = low(value)
    rest = value - high.astype(jnp.float32)
    middle = low(rest)
    tail = low(rest - middle.astype(jnp.float32))
    return jnp.stack([high, middle, tail])


def finish(direction, moment, weight, row_count):
    new_moment = MOMENTUM * moment + direction
    new_weight = weight - MATRIX_RATE / math.sqrt(row_count) * new_moment
    return (new_moment, new_weight)


def shards(
    characters,
    cotangent,
    lengths,
    vectors,
    vector_acc,
    attend_weight,
    attend_moment,
    attend_left,
    attend_right,
    attend_rootleft,
    attend_rootright,
    expand_weight,
    expand_moment,
    expand_left,
    expand_right,
    expand_rootleft,
    expand_rootright,
    shrink_weight,
    shrink_moment,
    shrink_left,
    shrink_right,
    shrink_rootleft,
    shrink_rootright,
):
    text_count, block_size, model_width = characters.shape
    token_rows = text_count * block_size
    both = ("seq", "dp")
    seq_count = lax.axis_size("seq")
    dp_count = lax.axis_size("dp")
    seq_index = lax.axis_index("seq")
    dp_index = lax.axis_index("dp")
    core = seq_index % 2
    chip = seq_index // 2
    tokens_all = token_rows * seq_count * dp_count
    grad_scale = 1.0 / math.sqrt(tokens_all)
    hidden = expand_weight.shape[1] * seq_count * dp_count
    part = hidden // seq_count
    block = model_width // (seq_count * dp_count)
    hidden_block = hidden // (seq_count * dp_count)
    rows_own = seq_count * block

    attend_t = attend_weight.transpose(1, 2, 0)
    expand_t = expand_weight.T
    shrink_t = shrink_weight.T
    shrink_cut = low(shrink_t).reshape(block, seq_count, part).transpose(1, 0, 2)
    packed = jnp.concatenate(
        [low(attend_t[3]), low(expand_t), shrink_cut.reshape(seq_count * block, part)]
    )
    packed_all = lax.all_gather(packed, both, axis=0)
    over_dp = spread(low(attend_t[:3]))
    over_chip = ordered(chip, over_dp, chip_swap(over_dp))
    over_core = ordered(core, over_chip, core_swap(over_chip))
    qkv_t = over_core.transpose(3, 1, 0, 2, 4, 5).reshape(3 * model_width, model_width)

    ends = seq_count - 1
    before = lax.ppermute(
        characters[:, block_size - WIN :], "seq", [(i, i + 1) for i in range(ends)]
    )
    after = lax.ppermute(characters[:, :WIN], "seq", [(i + 1, i) for i in range(ends)])
    input_ext = jnp.concatenate([before, characters, after], axis=1)
    wide = block_size + 2 * WIN

    gain_one = vectors[0]
    bias_one = vectors[1]
    query_bias = vectors[2]
    value_bias = vectors[3]
    out_bias = vectors[4]
    gain_two = vectors[5]
    bias_two = vectors[6]
    shrink_bias = vectors[7]
    expand_bias = vectors[8:].reshape(1, -1)
    normed_ext = low(normalize(input_ext.astype(jnp.float32), gain_one, bias_one))
    normed_low = normed_ext[:, WIN : WIN + block_size].reshape(token_rows, model_width)
    ext_rows = normed_ext.reshape(text_count * wide, model_width)
    query_low = low(nt(normed_low, qkv_t[:model_width]) + query_bias).reshape(characters.shape)
    key_ext = low(nt(ext_rows, qkv_t[model_width : 2 * model_width])).reshape(
        text_count, wide, model_width
    )
    value_ext = low(nt(ext_rows, qkv_t[2 * model_width :]) + value_bias).reshape(
        text_count, wide, model_width
    )
    base = (seq_index * block_size).astype(jnp.int32).reshape(1)
    attended, totals = run_forward(lengths, base, query_low, key_ext, value_ext)
    attended_low = attended.reshape(token_rows, model_width)

    out_t = packed_all[:, :block].reshape(model_width, model_width)
    expand_all = packed_all[:, block : block + hidden_block].reshape(hidden, model_width)
    shrink_all = (
        packed_all[:, block + hidden_block :]
        .reshape(seq_count * dp_count, seq_count, block, part)
        .transpose(0, 2, 1, 3)
        .reshape(model_width, hidden)
    )
    layer_input = characters.astype(jnp.float32).reshape(token_rows, model_width)
    middle = layer_input + nt(attended_low, out_t) + out_bias
    normed_two_low = low(normalize(middle, gain_two, bias_two))
    gated_low, slope_low = run_gate(normed_two_low, expand_all, expand_bias)
    layer_output = middle + nt(gated_low, shrink_all) + shrink_bias
    layer_output = low(layer_output).reshape(text_count, block_size, model_width)

    upstream = cotangent.reshape(token_rows, model_width)
    upstream_float = upstream.astype(jnp.float32)
    grad_shrink_bias = jnp.sum(upstream_float, axis=0)
    expanded_grad = low(nn(upstream, shrink_all) * slope_low.astype(jnp.float32))
    grad_expand_bias = jnp.sum(expanded_grad.astype(jnp.float32), axis=0)
    normed_two_grad = nn(expanded_grad, expand_all)

    def panel(rows, index):
        return rows[:, index * part : (index + 1) * part]

    def by_owner(one):
        return one.reshape(seq_count, dp_count, block, model_width).transpose(1, 0, 2, 3)

    def in_order(one):
        return one.reshape(dp_count, hidden_block, model_width)

    shrink_own = summed(
        [low(across(panel(gated_low, i), upstream)) for i in range(seq_count)],
        core,
        chip,
        in_order,
    )
    expand_own = summed(
        [low(across(normed_two_low, panel(expanded_grad, i))) for i in range(seq_count)],
        core,
        chip,
        by_owner,
    )
    unused_norm, norm_two_back = jax.vjp(normalize, middle, gain_two, bias_two)
    middle_part, grad_gain_two, grad_bias_two = norm_two_back(normed_two_grad)
    middle_grad = upstream_float + middle_part
    branch_grad = low(middle_grad)
    grad_out_bias = jnp.sum(branch_grad.astype(jnp.float32), axis=0)
    grad_out = low(across(attended_low, branch_grad))
    attended_grad = low(nn(branch_grad, out_t)).reshape(characters.shape)

    query_grad, key_grad, value_grad = run_backward(
        lengths, base, query_low, key_ext, value_ext, attended_grad, totals
    )
    pair_grad = jnp.stack([key_grad, value_grad])
    from_above = lax.ppermute(
        pair_grad[:, :, :WIN], "seq", [(i + 1, i) for i in range(ends)]
    )
    from_below = lax.ppermute(
        pair_grad[:, :, block_size + WIN :], "seq", [(i, i + 1) for i in range(ends)]
    )
    pair_own = pair_grad[:, :, WIN : WIN + block_size]
    pair_low = jnp.concatenate(
        [
            add_low(pair_own[:, :, :WIN], from_below),
            pair_own[:, :, WIN : block_size - WIN],
            add_low(pair_own[:, :, block_size - WIN :], from_above),
        ],
        axis=2,
    ).reshape(2, token_rows, model_width)
    query_rows = query_grad.reshape(token_rows, model_width)
    attend_own = summed(
        [
            low(across(normed_low, query_rows)),
            low(across(normed_low, pair_low[0])),
            low(across(normed_low, pair_low[1])),
            grad_out,
        ],
        core,
        chip,
        by_owner,
    )
    grad_query_bias = jnp.sum(query_rows.astype(jnp.float32), axis=0)
    grad_value_bias = jnp.sum(pair_low[1].astype(jnp.float32), axis=0)
    combined = jnp.concatenate([query_rows, pair_low[0], pair_low[1]], axis=1)
    normed_grad = nn(combined, qkv_t)
    unused_first, norm_one_back = jax.vjp(normalize, layer_input, gain_one, bias_one)
    input_part, grad_gain_one, grad_bias_one = norm_one_back(normed_grad)
    characters_grad = low(middle_grad + input_part).reshape(characters.shape)
    vector_terms = jnp.concatenate(
        [
            jnp.stack(
                [
                    grad_gain_one,
                    grad_bias_one,
                    grad_query_bias,
                    grad_value_bias,
                    grad_out_bias,
                    grad_gain_two,
                    grad_bias_two,
                    grad_shrink_bias,
                ]
            ),
            grad_expand_bias.reshape(-1, model_width),
        ],
        axis=0,
    )
    vector_sum = jnp.sum(lax.all_gather(vector_terms, both, axis=0), axis=0)
    vector_grad = vector_sum * grad_scale
    vector_newacc = vector_acc + vector_grad * vector_grad
    vector_new = vectors - VECTOR_RATE * vector_grad / (jnp.sqrt(vector_newacc) + 1e-08)

    expand_rt = low(expand_rootright.T).reshape(hidden_block, seq_count, part).transpose(1, 0, 2)
    shrink_lt = low(shrink_rootleft).reshape(hidden_block, seq_count, part).transpose(1, 0, 2)
    attend_lt = low(attend_rootleft).transpose(1, 0, 2)
    attend_rt = low(attend_rootright.transpose(1, 2, 0))
    roots = swap(jnp.concatenate([expand_rt, shrink_lt, attend_lt, attend_rt], axis=1))
    cut = 2 * hidden_block
    expand_rc = roots[:, :hidden_block].reshape(seq_count * hidden_block, part)
    shrink_lr = roots[:, hidden_block:cut].reshape(seq_count * hidden_block, part)
    attend_rc = roots[:, cut + block :].reshape(rows_own, model_width)
    attend_lw = lax.all_gather(
        roots[:, cut : cut + block], "dp", axis=1, tiled=True
    ).reshape(model_width, model_width)
    small = lax.all_gather(
        jnp.stack([low(expand_rootleft), low(shrink_rootright.T)]), both, axis=1, tiled=True
    )
    expand_lw = small[0]
    shrink_rt = small[1]

    shrink_own_low = low(shrink_own)
    expand_own_low = low(expand_own)
    panels = lax.all_gather(jnp.stack([shrink_own_low, expand_own_low.reshape(rows_own, part)]), "dp", axis=0)
    shrink_panel = panels[:, 0].reshape(part, model_width)
    shrink_sum = jnp.sum(jnp.square(shrink_panel.astype(jnp.float32)))
    expand_panel = (
        panels[:, 1]
        .reshape(dp_count, seq_count, block, part)
        .transpose(1, 0, 2, 3)
        .reshape(model_width, part)
    )
    expand_sum = jnp.sum(jnp.square(expand_panel.astype(jnp.float32)))
    expand_cols = lax.dynamic_slice_in_dim(expand_panel, dp_index * hidden_block, hidden_block, 1).T
    sums = jnp.broadcast_to(
        jnp.concatenate([thirds(shrink_sum), thirds(expand_sum), jnp.zeros((10,), jnp.bfloat16)])[
            :, None
        ],
        (16, model_width),
    )
    mixed = lax.all_gather(jnp.concatenate([shrink_own_low, expand_cols, sums]), "seq", axis=0)
    shrink_rows = mixed[:, :hidden_block].reshape(seq_count * hidden_block, model_width)
    expand_colset = mixed[:, hidden_block:cut].reshape(seq_count * hidden_block, model_width)
    totals = jnp.sum(mixed[:, cut : cut + 6, 0].astype(jnp.float32), axis=0)
    count_all = model_width * hidden
    square_scale = grad_scale * grad_scale
    shrink_square = jnp.sum(totals[:3]) * square_scale / count_all + STAT_EPSILON
    expand_square = jnp.sum(totals[3:]) * square_scale / count_all + STAT_EPSILON

    def col_set(panel):
        picked = lax.dynamic_slice_in_dim(
            panel.reshape(panel.shape[0], seq_count, dp_count, block), dp_index, 1, 2
        )
        return picked.reshape(panel.shape[0], rows_own)

    shrink_left_new = nt(shrink_rows, shrink_panel).reshape(seq_count, hidden_block, part)
    shrink_right_new = across(col_set(shrink_panel), shrink_panel).reshape(
        seq_count, block, model_width
    )
    shrink_applied = nn(shrink_lr, shrink_panel).reshape(seq_count, hidden_block, model_width)
    expand_right_new = nn(expand_colset, expand_panel).reshape(seq_count, hidden_block, part)
    expand_left_new = nt(expand_own_low.reshape(rows_own, part), expand_panel).reshape(
        seq_count, block, model_width
    )
    expand_applied = nt(expand_rc, expand_panel).reshape(seq_count, hidden_block, model_width)
    back = swap(
        jnp.concatenate(
            [
                low(shrink_left_new),
                low(shrink_applied),
                low(expand_right_new),
                low(expand_applied),
                low(shrink_right_new),
                low(expand_left_new),
                expand_own_low,
            ],
            axis=1,
        )
    )
    parts = []
    start = 0
    for width in [hidden_block] * 4 + [block] * 3:
        parts.append(back[:, start : start + width])
        start += width

    def unfold(blocks):
        return blocks.transpose(1, 0, 2).reshape(blocks.shape[1], -1)

    def total(blocks):
        return jnp.sum(blocks.astype(jnp.float32), axis=0)

    shrink_scale = square_scale / shrink_square
    expand_scale = square_scale / expand_square
    shrink_newleft = 0.5 * shrink_left + unfold(parts[0]).astype(jnp.float32) * (
        0.5 * shrink_scale / model_width
    )
    shrink_newright_t = 0.5 * shrink_right.T + total(parts[4]) * (0.5 * shrink_scale / hidden)
    expand_newright_t = 0.5 * expand_right.T + unfold(parts[2]).astype(jnp.float32) * (
        0.5 * expand_scale / model_width
    )
    expand_newleft = 0.5 * expand_left + total(parts[5]) * (0.5 * expand_scale / hidden)
    expand_rows = unfold(parts[6]).astype(jnp.float32) * grad_scale
    expand_direction_t = nt(low(total(parts[3])), expand_lw) * (
        grad_scale * lax.rsqrt(expand_square)
    )
    shrink_turned = nt(shrink_rt, low(total(parts[1])))
    shrink_direction_t = (
        lax.all_to_all(
            low(shrink_turned).reshape(seq_count * dp_count, block, hidden_block),
            both,
            split_axis=0,
            concat_axis=0,
            tiled=True,
        )
        .transpose(1, 0, 2)
        .reshape(block, hidden)
        .astype(jnp.float32)
    ) * (grad_scale * lax.rsqrt(shrink_square))
    expand_newmoment_t, expand_newweight_t = finish(
        expand_direction_t, expand_moment.T, expand_t, model_width
    )
    shrink_newmoment_t, shrink_newweight_t = finish(
        shrink_direction_t, shrink_moment.T, shrink_t, hidden
    )

    attend_own_low = low(attend_own)
    whole = (
        spread(attend_own_low).transpose(1, 0, 2, 3).reshape(model_width, model_width)
    )
    attend_square = (
        jnp.mean(jnp.square(whole.astype(jnp.float32))) * square_scale + STAT_EPSILON
    )
    gram_scale = 0.5 * square_scale / attend_square / model_width
    attend_left_new = nt(attend_own_low.reshape(rows_own, model_width), whole) * gram_scale
    attend_right_new = across(col_set(whole), whole) * gram_scale
    attend_turned = nt(low(nt(attend_rc, whole)), attend_lw) * (
        grad_scale * lax.rsqrt(attend_square)
    )
    returned = swap(
        jnp.concatenate(
            [
                low(attend_left_new).reshape(seq_count, block, model_width),
                low(attend_right_new).reshape(seq_count, block, model_width),
                low(attend_turned).reshape(seq_count, block, model_width),
                attend_own_low,
            ],
            axis=1,
        )
    ).astype(jnp.float32)
    attend_newleft = 0.5 * attend_left + returned[:, :block].transpose(1, 0, 2)
    attend_newright_t = 0.5 * attend_right.transpose(1, 2, 0) + returned[:, block : 2 * block]
    attend_direction_t = returned[:, 2 * block : 3 * block]
    attend_rows = returned[:, 3 * block :].transpose(1, 0, 2) * grad_scale
    attend_newmoment_t, attend_newweight_t = finish(
        attend_direction_t, attend_moment.transpose(1, 2, 0), attend_t, model_width
    )
    shrink_grad = shrink_own * grad_scale
    return (
        layer_output,
        characters_grad,
        attend_rows,
        attend_newmoment_t.transpose(2, 0, 1),
        attend_newweight_t.transpose(2, 0, 1),
        attend_newleft,
        attend_newright_t.transpose(2, 0, 1),
        expand_rows,
        expand_newmoment_t.T,
        expand_newweight_t.T,
        expand_newleft,
        expand_newright_t.T,
        shrink_grad,
        shrink_newmoment_t.T,
        shrink_newweight_t.T,
        shrink_newleft,
        shrink_newright_t.T,
        vector_grad,
        vector_newacc,
        vector_new,
    )


def solution(mesh):
    return jax.shard_map(
        shards,
        mesh=mesh,
        in_specs=(
            P("dp", "seq", None),
            P("dp", "seq", None),
            P("dp"),
            P(),
            P(),
            P(None, None, ("seq", "dp")),
            P(None, None, ("seq", "dp")),
            P(("seq", "dp"), None, None),
            P(None, None, ("seq", "dp")),
            P(("seq", "dp"), None, None),
            P(None, None, ("seq", "dp")),
            P(None, ("seq", "dp")),
            P(None, ("seq", "dp")),
            P(("seq", "dp"), None),
            P(None, ("seq", "dp")),
            P(("seq", "dp"), None),
            P(None, ("seq", "dp")),
            P(None, ("seq", "dp")),
            P(None, ("seq", "dp")),
            P(("seq", "dp"), None),
            P(None, ("seq", "dp")),
            P(("seq", "dp"), None),
            P(None, ("seq", "dp")),
        ),
        out_specs=(
            P("dp", "seq", None),
            P("dp", "seq", None),
            P(("seq", "dp"), None, None),
            P(None, None, ("seq", "dp")),
            P(None, None, ("seq", "dp")),
            P(("seq", "dp"), None, None),
            P(None, None, ("seq", "dp")),
            P(("seq", "dp"), None),
            P(None, ("seq", "dp")),
            P(None, ("seq", "dp")),
            P(("seq", "dp"), None),
            P(None, ("seq", "dp")),
            P(("seq", "dp"), None),
            P(None, ("seq", "dp")),
            P(None, ("seq", "dp")),
            P(("seq", "dp"), None),
            P(None, ("seq", "dp")),
            P(),
            P(),
            P(),
        ),
        check_vma=False,
    )
```

```python
import functools
import math

import jax
import jax.numpy as jnp
from jax import lax
from jax.experimental import pallas as pl
from jax.experimental.pallas import tpu as pltpu
from jax.sharding import PartitionSpec as P

HEAD = 64
WIN = 128
PAIR = 2 * HEAD
KEYS = 3 * WIN
VMEM_BYTES = 56 * 1024 * 1024

EPSILON = 1e-05
STAT_EPSILON = 1e-06
MATRIX_RATE = 0.5
VECTOR_RATE = 0.3
MOMENTUM = 0.9
MASKED = -1e30

PHI_POLY = (
    0.7978849414608439,
    0.03633308457157131,
    -3.259497261642231e-05,
    -5.530619510506789e-05,
    3.964744703196676e-06,
    -1.3226336477723372e-07,
    1.7561715138424972e-09,
)


def nt(left_rows, right_rows):
    return lax.dot_general(
        left_rows, right_rows, (((1,), (1,)), ((), ())), preferred_element_type=jnp.float32
    )


def nn(left_rows, right_cols):
    return jnp.dot(left_rows, right_cols, preferred_element_type=jnp.float32)


def across(left_rows, right_rows):
    return lax.dot_general(
        left_rows, right_rows, (((0,), (0,)), ((), ())), preferred_element_type=jnp.float32
    )


def low(values):
    return values.astype(jnp.bfloat16)


def normalize(values, gain_row, bias_row):
    centre = values - jnp.mean(values, axis=-1, keepdims=True)
    spread = jnp.mean(centre * centre, axis=-1, keepdims=True)
    return centre * lax.rsqrt(spread + EPSILON) * gain_row + bias_row


def params():
    return pltpu.CompilerParams(vmem_limit_bytes=VMEM_BYTES)


def write_mask(bias_ref, length, base, blocks):
    for i in range(blocks):
        key = lax.broadcasted_iota(jnp.int32, (KEYS, WIN), 0)
        query = lax.broadcasted_iota(jnp.int32, (KEYS, WIN), 1)
        place = key + (base + (i - 1) * WIN)
        near = (key >= query) & (key <= query + 2 * WIN)
        seen = ((place >= 0) & (place < length)) | (key == query + WIN)
        bias_ref[i] = jnp.where(near & seen, 0.0, MASKED)


def stacked(rows, scale):
    lane = lax.broadcasted_iota(jnp.int32, rows.shape, 1)
    rows = rows.astype(jnp.float32) * scale
    first = jnp.where(lane < HEAD, rows, 0.0)
    second = jnp.where(lane < HEAD, 0.0, rows)
    return low(jnp.concatenate([first, second], axis=0))


def unstacked(turned):
    pair = jnp.concatenate([turned[:HEAD, :WIN], turned[HEAD:, WIN:]], axis=0)
    return pair.T


def attend_forward(blocks, lengths, base, q_ref, k_ref, v_ref, o_ref, total_ref, bias_ref):
    text = pl.program_id(0)

    @pl.when(pl.program_id(1) == 0)
    def _():
        write_mask(bias_ref, lengths[text], base[0], blocks)

    for i in range(blocks):
        keys = k_ref[0, i * WIN : i * WIN + KEYS, :]
        values = v_ref[0, i * WIN : i * WIN + KEYS, :]
        queries = stacked(q_ref[0, i * WIN : (i + 1) * WIN, :], 0.125)
        bias = bias_ref[i]
        scores = nt(keys, queries) + jnp.concatenate([bias, bias], axis=1)
        peak = jnp.max(scores, axis=0, keepdims=True)
        weights = jnp.exp(scores - peak)
        total = jnp.sum(weights, axis=0, keepdims=True)
        mixed = across(values, low(weights)) * (1.0 / total)
        o_ref[0, i * WIN : (i + 1) * WIN, :] = low(unstacked(mixed))
        log_total = peak + jnp.log(total)
        total_ref[0, 0, 2 * i : 2 * i + 1, :] = log_total[:, :WIN]
        total_ref[0, 0, 2 * i + 1 : 2 * i + 2, :] = log_total[:, WIN:]


def attend_backward(
    blocks,
    extra,
    lengths,
    base,
    q_ref,
    k_ref,
    v_ref,
    up_ref,
    total_ref,
    *rest,
):
    dq_ref, dk_ref, dv_ref, bias_ref, dk_sum, dv_sum = rest[extra:]
    text = pl.program_id(0)

    @pl.when(pl.program_id(1) == 0)
    def _():
        write_mask(bias_ref, lengths[text], base[0], blocks)

    dk_sum[...] = jnp.zeros_like(dk_sum)
    dv_sum[...] = jnp.zeros_like(dv_sum)
    for i in range(blocks):
        window = slice(i * WIN, i * WIN + KEYS)
        own = slice(i * WIN, (i + 1) * WIN)
        keys = k_ref[0, window, :]
        values = v_ref[0, window, :]
        queries = stacked(q_ref[0, own, :], 0.125)
        upstream = stacked(up_ref[0, own, :], 1.0)
        bias = bias_ref[i]
        log_total = jnp.concatenate(
            [total_ref[0, 0, 2 * i : 2 * i + 1, :], total_ref[0, 0, 2 * i + 1 : 2 * i + 2, :]],
            axis=1,
        )
        scores = nt(keys, queries) + jnp.concatenate([bias, bias], axis=1)
        weights = jnp.exp(scores - log_total)
        weight_grad = nt(values, upstream)
        product = weights * weight_grad
        score_grad = low(product - weights * jnp.sum(product, axis=0, keepdims=True))
        dv_sum[window, :] += nn(low(weights), upstream)
        dk_sum[window, :] += nn(score_grad, queries)
        dq_ref[0, own, :] = low(unstacked(across(keys, score_grad)) * 0.125)
    dk_ref[0] = low(dk_sum[...])
    dv_ref[0] = low(dv_sum[...])


def attention_specs(block_size):
    wide = block_size + 2 * WIN
    blocks = block_size // WIN
    own = pl.BlockSpec((1, block_size, PAIR), lambda t, g: (t, 0, g))
    ext = pl.BlockSpec((1, wide, PAIR), lambda t, g: (t, 0, g))
    sums = pl.BlockSpec((1, 1, 2 * blocks, WIN), lambda t, g: (t, g, 0, 0))
    smem = pl.BlockSpec(memory_space=pltpu.SMEM)
    return wide, blocks, own, ext, sums, smem


def run_forward(lengths, base, query, key_ext, value_ext):
    texts, block_size, width = query.shape
    wide, blocks, own, ext, sums, smem = attention_specs(block_size)
    work = texts * blocks * (width // PAIR)
    return pl.pallas_call(
        functools.partial(attend_forward, blocks),
        grid=(texts, width // PAIR),
        in_specs=[smem, smem, own, ext, ext],
        out_specs=[own, sums],
        out_shape=[
            jax.ShapeDtypeStruct(query.shape, jnp.bfloat16),
            jax.ShapeDtypeStruct((texts, width // PAIR, 2 * blocks, WIN), jnp.float32),
        ],
        scratch_shapes=[pltpu.VMEM((blocks, KEYS, WIN), jnp.float32)],
        compiler_params=params(),
        cost_estimate=pl.CostEstimate(
            flops=work * 4 * KEYS * PAIR * 2 * WIN,
            bytes_accessed=query.size * 2 * 5,
            transcendentals=work * KEYS * 2 * WIN,
        ),
        name="attend_forward",
    )(lengths, base, query, key_ext, value_ext)


def run_backward(pairs, lengths, base, query, key_ext, value_ext, upstream, totals, kept, first):
    texts, block_size, width = query.shape
    wide = block_size + 2 * WIN
    blocks = block_size // WIN
    low_pair, count = pairs
    own = pl.BlockSpec((1, block_size, PAIR), lambda t, g: (t, 0, low_pair + g))
    ext = pl.BlockSpec((1, wide, PAIR), lambda t, g: (t, 0, low_pair + g))
    sums = pl.BlockSpec((1, 1, 2 * blocks, WIN), lambda t, g: (t, low_pair + g, 0, 0))
    smem = pl.BlockSpec(memory_space=pltpu.SMEM)
    others = tuple(kept) + tuple(first)
    work = texts * blocks * count
    return pl.pallas_call(
        functools.partial(attend_backward, blocks, len(others)),
        grid=(texts, count),
        in_specs=[smem, smem, own, ext, ext, own, sums]
        + [pl.BlockSpec(memory_space=pl.ANY)] * len(others),
        out_specs=[own, ext, ext],
        out_shape=[
            jax.ShapeDtypeStruct(query.shape, jnp.bfloat16),
            jax.ShapeDtypeStruct(key_ext.shape, jnp.bfloat16),
            jax.ShapeDtypeStruct(key_ext.shape, jnp.bfloat16),
        ],
        scratch_shapes=[
            pltpu.VMEM((blocks, KEYS, WIN), jnp.float32),
            pltpu.VMEM((wide, PAIR), jnp.float32),
            pltpu.VMEM((wide, PAIR), jnp.float32),
        ],
        input_output_aliases={7 + i: i for i in range(len(kept))},
        compiler_params=params(),
        cost_estimate=pl.CostEstimate(
            flops=work * 10 * KEYS * PAIR * 2 * WIN,
            bytes_accessed=query.size * 10,
            transcendentals=work * KEYS * 2 * WIN,
        ),
        name="attend_backward",
    )(lengths, base, query, key_ext, value_ext, upstream, totals, *others)


GATE_ROWS = 256
GATE_COLS = 256
GATE_SLAB = 32
BELL = 1.0 / math.sqrt(2.0 * math.pi)


def gate_kernel(
    rows_ref,
    upstream_ref,
    in_ref,
    out_ref,
    bias_ref,
    gate_ref,
    grad_ref,
    sums_ref,
    forward_ref,
    back_ref,
    forward_sum,
    back_sum,
):
    panel, tile = pl.program_id(0), pl.program_id(1)
    part = rows_ref.shape[1]
    ones = jnp.ones((8, GATE_ROWS), jnp.bfloat16)
    chunks = part // GATE_COLS

    def products(c):
        cols = slice(c * GATE_COLS, (c + 1) * GATE_COLS)
        hidden = nt(rows_ref[...], in_ref[cols, :]) + bias_ref[:, cols]
        return hidden, nn(upstream_ref[...], out_ref[:, cols])

    later = products(0)
    for c in range(chunks):
        hidden, hidden_grad = later
        if c + 1 < chunks:
            later = products(c + 1)
        cols = slice(c * GATE_COLS, (c + 1) * GATE_COLS)
        for i in range(GATE_ROWS // GATE_SLAB):
            own = slice(i * GATE_SLAB, (i + 1) * GATE_SLAB)
            u = hidden[own, :]
            square = u * u
            poly = PHI_POLY[-1] * square + PHI_POLY[-2]
            for term in PHI_POLY[-3::-1]:
                poly = poly * square + term
            half = 0.5 * jnp.tanh(poly * u)
            phi = half + 0.5
            bell = jnp.exp2(square * (-0.5 * math.log2(math.e)))
            gate_ref[own, cols] = low(u * phi)
            grad_ref[own, cols] = low(hidden_grad[own, :] * (phi + (u * BELL) * bell))
        sums_ref[0, :, cols] = nn(ones, grad_ref[:, cols])
    slot = pl.ds(pl.multiple_of(tile * GATE_ROWS, GATE_ROWS), GATE_ROWS)
    forward = nt(gate_ref[...], out_ref[...])
    back = nn(grad_ref[...], in_ref[...])

    @pl.when(panel == 0)
    def _():
        forward_sum[slot, :] = forward
        back_sum[slot, :] = back

    @pl.when(panel > 0)
    def _():
        forward_sum[slot, :] += forward
        back_sum[slot, :] += back

    @pl.when(panel == pl.num_programs(0) - 1)
    def _():
        forward_ref[...] = forward_sum[slot, :]
        back_ref[...] = back_sum[slot, :]


def run_gate(rows, upstream, packed, bias):
    tokens, width = rows.shape
    hidden = bias.shape[1]
    groups = hidden // width
    tiles = tokens // GATE_ROWS
    row_spec = pl.BlockSpec((GATE_ROWS, width), lambda j, i: (i, 0))
    out_spec = pl.BlockSpec((GATE_ROWS, width), lambda j, i: (i, j))
    last_spec = pl.BlockSpec(
        (GATE_ROWS, width), lambda j, i: (jnp.where(j == groups - 1, i, 0), 0)
    )
    wide_out = jax.ShapeDtypeStruct((tokens, hidden), jnp.bfloat16)
    row_out = jax.ShapeDtypeStruct((tokens, width), jnp.float32)
    return pl.pallas_call(
        gate_kernel,
        grid=(groups, tiles),
        in_specs=[
            row_spec,
            row_spec,
            pl.BlockSpec((width, width), lambda j, i: (0, 1 + groups + j)),
            pl.BlockSpec((width, width), lambda j, i: (0, 1 + j)),
            pl.BlockSpec((1, width), lambda j, i: (0, j)),
        ],
        out_specs=[
            out_spec,
            out_spec,
            pl.BlockSpec((1, 8, width), lambda j, i: (i, 0, j)),
            last_spec,
            last_spec,
        ],
        out_shape=[
            wide_out,
            wide_out,
            jax.ShapeDtypeStruct((tiles, 8, hidden), jnp.float32),
            row_out,
            row_out,
        ],
        scratch_shapes=[pltpu.VMEM((tokens, width), jnp.float32)] * 2,
        compiler_params=params(),
        cost_estimate=pl.CostEstimate(
            flops=tokens * width * hidden,
            bytes_accessed=4 * (tokens * width + width * hidden + tokens * hidden),
            transcendentals=2 * tokens * hidden,
        ),
        name="gate",
    )(rows, upstream, packed, packed, bias)


def flip(blocks, axis, mask):
    count = lax.axis_size(axis)
    return lax.ppermute(blocks, axis, [(i, i ^ mask) for i in range(count)])


def swap(blocks):
    return lax.all_to_all(blocks, "seq", split_axis=0, concat_axis=0, tiled=True)


def spread(block, axis="dp"):
    copies = jnp.broadcast_to(block[None], (lax.axis_size(axis),) + block.shape)
    return lax.all_to_all(copies, axis, split_axis=0, concat_axis=0, tiled=True)


def ordered(bit, own, other, dim):
    return jnp.where(
        bit == 0, jnp.stack([own, other], axis=dim), jnp.stack([other, own], axis=dim)
    )


def after(value, *first):
    return lax.optimization_barrier((value,) + first)[0]


def add_low(left, right):
    return low(left.astype(jnp.float32) + right.astype(jnp.float32))


def dp_bits():
    return lax.axis_size("dp").bit_length() - 1


class Halving:
    def __init__(self, blocks, dims):
        self.blocks, self.dims = blocks, list(dims)

    def start(self, dim):
        place = self.dims.index(dim)
        axis, shift = ("seq", "cx".index(dim)) if isinstance(dim, str) else ("dp", dim)
        bit = lax.axis_index(axis) // (1 << shift) % 2
        sent = lax.dynamic_index_in_dim(self.blocks, 1 - bit, place, keepdims=False)
        self.kept = lax.dynamic_index_in_dim(self.blocks, bit, place, keepdims=False)
        self.got = flip(sent, axis, 1 << shift)
        self.dims.pop(place)

    def finish(self, last=False, first=None):
        got = self.got if first is None else after(self.got, first)
        total = self.kept.astype(jnp.float32) + got.astype(jnp.float32)
        self.blocks = total if last else low(total)


def rounds():
    bits = list(range(dp_bits()))
    return list(zip(["x"] + bits, bits + ["x"]))


def one_round(one, other, i, first=None):
    left, right = rounds()[i]
    last = i == len(rounds()) - 1
    one.start(left)
    other.start(right)
    one.finish(last, first)
    other.finish(last, first)
    return [mark(one.blocks), mark(other.blocks)]


def mark(array):
    return array.reshape(-1, array.shape[-1])[:8, :128]


def picker(count, block, dp_count, dp_index, width):
    row = lax.broadcasted_iota(jnp.int32, (count * block, width), 0)
    col = lax.broadcasted_iota(jnp.int32, (count * block, width), 1)
    found = jnp.zeros(row.shape, jnp.float32)
    for s in range(count):
        here = (row >= s * block) & (row < (s + 1) * block)
        place = row + (s * (dp_count - 1) + dp_index) * block
        found = jnp.where(here & (col == place), 1.0, found)
    return low(found)


def padded(rows):
    extra = -rows.shape[0] % 16
    if extra:
        rows = jnp.concatenate([rows, jnp.zeros((extra, rows.shape[1]), jnp.float32)])
    return low(rows)


def hidden_first(seq_count, block, dp_count, dp_index, panels, row_sets, expand_rc, shrink_rc, expand_lw):
    shrink, expand = panels[0], panels[1]
    width = shrink.shape[0]
    pick = picker(seq_count, block, dp_count, dp_index, width)
    shrink_cols = low(nt(pick, shrink))
    expand_cols = nt(pick, expand)
    turned = low(nt(shrink_rc, shrink))
    shrink_right = nn(shrink_cols, shrink)
    expand_left = nn(low(expand_cols), expand)
    expand_turned = nt(low(nn(expand_rc, expand)), expand_lw)
    owned = expand_rc.shape[0] // seq_count
    sums = [
        jnp.sum(jnp.sum(jnp.square(p.astype(jnp.float32)), axis=0, keepdims=True), axis=1, keepdims=True)
        for p in (shrink, expand)
    ]
    line = lax.broadcasted_iota(jnp.int32, (16, width), 0)
    marks = jnp.zeros((16, width), jnp.float32)
    for i, value in enumerate(sums):
        for j in range(3):
            piece = low(jnp.broadcast_to(value, (16, width))).astype(jnp.float32)
            marks = jnp.where(line == 3 * i + j, piece, marks)
            value = value - piece[:1, :1]
    pieces = []
    for s in range(seq_count):
        rows = slice(s * owned, (s + 1) * owned)
        few = slice(s * block, (s + 1) * block)
        pieces.append(
            [
                padded(nt(row_sets[s, 0], shrink)),
                padded(nt(row_sets[s, 1], expand)),
                padded(expand_turned[rows]),
                padded(shrink_right[few]),
                padded(expand_left[few]),
                padded(expand_cols[few]),
                low(marks),
            ]
        )
    return pieces, turned


def direction_rows(seq_count, block, turned, shrink_lw):
    rows = nt(turned, shrink_lw)
    return [rows[s * block : (s + 1) * block] for s in range(seq_count)]


def hidden_kernel(
    seq_count,
    block,
    dp_count,
    index_ref,
    panels_ref,
    rows_ref,
    expand_rc_ref,
    shrink_rc_ref,
    expand_lw_ref,
    shrink_lw_ref,
    token_ref,
    out_ref,
    turn_ref,
    turned_ref,
):
    step = pl.program_id(0)

    @pl.when(step == 0)
    def _():
        pieces, turned = hidden_first(
            seq_count,
            block,
            dp_count,
            index_ref[0],
            panels_ref,
            rows_ref,
            expand_rc_ref[...],
            shrink_rc_ref[...],
            expand_lw_ref[...],
        )
        turned_ref[...] = turned
        for s in range(seq_count):
            start = 0
            for piece in pieces[s]:
                out_ref[s, start : start + piece.shape[0], :] = piece
                start += piece.shape[0]

    for s, rows in enumerate(direction_rows(seq_count, block, turned_ref[...], shrink_lw_ref[0])):
        turn_ref[s, 0] = padded(rows)


def run_hidden(seq_count, block, dp_count, dp_index, panels, row_sets, rc, shrink_rc, lw, shrink_lw, token):
    width = panels.shape[1]
    groups = shrink_lw.shape[0]
    owned = rc.shape[0] // seq_count
    if owned % 16 or block % 8:
        pieces, turned = hidden_first(
            seq_count, block, dp_count, dp_index, panels, row_sets, rc, shrink_rc, lw
        )
        turns = [direction_rows(seq_count, block, turned, shrink_lw[i]) for i in range(groups)]
        return (
            jnp.stack([jnp.concatenate(piece) for piece in pieces]),
            jnp.stack(
                [jnp.stack([padded(turns[i][s]) for i in range(groups)]) for s in range(seq_count)]
            ),
        )
    few = block + -block % 16
    rows_out = 3 * owned + 3 * few + 16
    whole = lambda array: pl.BlockSpec(array.shape, lambda i: (0,) * array.ndim)
    return pl.pallas_call(
        functools.partial(hidden_kernel, seq_count, block, dp_count),
        grid=(groups,),
        in_specs=[
            pl.BlockSpec(memory_space=pltpu.SMEM),
            whole(panels),
            whole(row_sets),
            whole(rc),
            whole(shrink_rc),
            whole(lw),
            pl.BlockSpec((1, width, width), lambda i: (i, 0, 0)),
            pl.BlockSpec(memory_space=pl.ANY),
        ],
        out_specs=[
            pl.BlockSpec((seq_count, rows_out, width), lambda i: (0, 0, 0)),
            pl.BlockSpec((seq_count, 1, few, width), lambda i: (0, i, 0, 0)),
        ],
        out_shape=[
            jax.ShapeDtypeStruct((seq_count, rows_out, width), jnp.bfloat16),
            jax.ShapeDtypeStruct((seq_count, groups, few, width), jnp.bfloat16),
        ],
        scratch_shapes=[pltpu.VMEM(shrink_rc.shape, jnp.bfloat16)],
        compiler_params=params(),
        cost_estimate=pl.CostEstimate(
            flops=40 * owned * width * width, bytes_accessed=12 * width * width, transcendentals=0
        ),
        name="hidden_update",
    )(dp_index.reshape(1), panels, row_sets, rc, shrink_rc, lw, shrink_lw, token)


def attend_products(seq_count, block, dp_count, dp_index, scale, whole, own, rc, lw):
    width = whole.shape[0]
    pick = picker(seq_count, block, dp_count, dp_index, width)
    wide = whole.astype(jnp.float32)
    total = jnp.sum(jnp.sum(wide * wide, axis=0, keepdims=True), axis=1, keepdims=True)
    square = total * (scale * scale / (width * width)) + STAT_EPSILON
    gram = (0.5 * scale * scale / width) / square
    left = nt(low(own), whole) * gram
    right = nn(low(nt(pick, whole)), whole) * gram
    turned = nt(low(nt(rc, whole)), lw) * (scale * lax.rsqrt(square))
    return [
        [padded(piece[s * block : (s + 1) * block]) for piece in (left, right, turned, own)]
        for s in range(seq_count)
    ]


def attend_kernel(seq_count, block, dp_count, scale, index_ref, whole_ref, own_ref, rc_ref, lw_ref, token_ref, out_ref):
    pieces = attend_products(
        seq_count,
        block,
        dp_count,
        index_ref[0],
        scale,
        whole_ref[...],
        own_ref[...],
        rc_ref[...],
        lw_ref[...],
    )
    for s in range(seq_count):
        for i, piece in enumerate(pieces[s]):
            out_ref[s, i] = piece


def run_attend(seq_count, block, dp_count, dp_index, scale, whole, own, rc, lw, token):
    width = whole.shape[0]
    if block % 8:
        pieces = attend_products(
            seq_count, block, dp_count, dp_index, scale, whole, own, rc, lw
        )
        return jnp.stack([jnp.stack(piece) for piece in pieces])
    few = block + -block % 16
    vmem = pl.BlockSpec(memory_space=pltpu.VMEM)
    return pl.pallas_call(
        functools.partial(attend_kernel, seq_count, block, dp_count, scale),
        in_specs=[pl.BlockSpec(memory_space=pltpu.SMEM)]
        + [vmem] * 4
        + [pl.BlockSpec(memory_space=pl.ANY)],
        out_specs=vmem,
        out_shape=jax.ShapeDtypeStruct((seq_count, 4, few, width), jnp.bfloat16),
        compiler_params=params(),
        cost_estimate=pl.CostEstimate(
            flops=10 * own.shape[0] * width * width, bytes_accessed=6 * width * width, transcendentals=0
        ),
        name="attend_update",
    )(dp_index.reshape(1), whole, own, rc, lw, token)


def finish(direction, moment, weight, row_count):
    new_moment = MOMENTUM * moment + direction
    new_weight = weight - MATRIX_RATE / math.sqrt(row_count) * new_moment
    return (new_moment, new_weight)


def shards(
    characters,
    cotangent,
    lengths,
    vectors,
    vector_acc,
    attend_weight,
    attend_moment,
    attend_left,
    attend_right,
    attend_rootleft,
    attend_rootright,
    expand_weight,
    expand_moment,
    expand_left,
    expand_right,
    expand_rootleft,
    expand_rootright,
    shrink_weight,
    shrink_moment,
    shrink_left,
    shrink_right,
    shrink_rootleft,
    shrink_rootright,
):
    text_count, block_size, model_width = characters.shape
    token_rows = text_count * block_size
    both = ("seq", "dp")
    seq_count = lax.axis_size("seq")
    dp_count = lax.axis_size("dp")
    seq_index = lax.axis_index("seq")
    dp_index = lax.axis_index("dp")
    core = seq_index % 2
    chip = seq_index // 2
    tokens_all = token_rows * seq_count * dp_count
    grad_scale = 1.0 / math.sqrt(tokens_all)
    square_scale = grad_scale * grad_scale
    hidden = expand_weight.shape[1] * seq_count * dp_count
    part = hidden // seq_count
    block = model_width // (seq_count * dp_count)
    hidden_block = hidden // (seq_count * dp_count)
    rows_own = seq_count * block

    owners = seq_count * dp_count
    groups = hidden // model_width
    ends = seq_count - 1
    before = lax.ppermute(
        characters[:, block_size - WIN :], "seq", [(i, i + 1) for i in range(ends)]
    )
    follow = lax.ppermute(characters[:, :WIN], "seq", [(i + 1, i) for i in range(ends)])

    attend_t = attend_weight.transpose(1, 2, 0)
    expand_t = expand_weight.T
    shrink_t = shrink_weight.T
    packed = jnp.concatenate(
        [
            low(attend_t[3]),
            low(shrink_t)
            .reshape(block, owners, groups, block)
            .transpose(0, 2, 1, 3)
            .reshape(block, hidden),
            low(expand_t)
            .reshape(groups, block, model_width)
            .transpose(1, 0, 2)
            .reshape(block, hidden),
        ],
        axis=1,
    )
    packed_all = lax.all_gather(packed, both, axis=0, tiled=True)
    over_dp = spread(low(attend_t[:3])).transpose(1, 0, 2, 3)

    def panels_of(rows):
        return low(rows).reshape(rows.shape[0], seq_count, part).transpose(1, 0, 2)

    def copies_of(rows):
        return jnp.broadcast_to(low(rows)[None], (seq_count,) + rows.shape)

    root_parts = jnp.concatenate(
        [
            panels_of(expand_rootright.T),
            low(attend_rootright.transpose(1, 2, 0)),
            copies_of(shrink_rootright.T),
            panels_of(shrink_rootleft),
            low(attend_rootleft).transpose(1, 0, 2),
            copies_of(expand_rootleft),
        ],
        axis=1,
    )
    over_chip = ordered(chip, over_dp, flip(over_dp, "seq", 2), 1)

    input_ext = jnp.concatenate([before, characters, follow], axis=1)
    wide = block_size + 2 * WIN

    gain_one = vectors[0]
    bias_one = vectors[1]
    query_bias = vectors[2]
    value_bias = vectors[3]
    out_bias = vectors[4]
    gain_two = vectors[5]
    bias_two = vectors[6]
    shrink_bias = vectors[7]
    expand_bias = vectors[8:].reshape(owners, groups, block).transpose(1, 0, 2).reshape(1, -1)
    normed_ext = low(normalize(input_ext.astype(jnp.float32), gain_one, bias_one))
    over_chip, normed_ext, root_parts = lax.optimization_barrier(
        (over_chip, normed_ext, root_parts)
    )
    over_core = ordered(core, over_chip, flip(over_chip, "seq", 1), 2)
    qkv_t = over_core.reshape(3 * model_width, model_width)
    roots = swap(root_parts)
    normed_low = normed_ext[:, WIN : WIN + block_size].reshape(token_rows, model_width)
    ext_rows = normed_ext.reshape(text_count * wide, model_width)
    query_low = low(nt(normed_low, qkv_t[:model_width]) + query_bias).reshape(characters.shape)
    key_ext = low(nt(ext_rows, qkv_t[model_width : 2 * model_width])).reshape(
        text_count, wide, model_width
    )
    value_ext = low(nt(ext_rows, qkv_t[2 * model_width :]) + value_bias).reshape(
        text_count, wide, model_width
    )
    query_low, roots = lax.optimization_barrier((query_low, roots))
    cut = hidden_block + 2 * block
    root_all = lax.all_gather(roots[:, cut:], "dp", axis=1)
    base = (seq_index * block_size).astype(jnp.int32).reshape(1)
    attended, totals = run_forward(lengths, base, query_low, key_ext, value_ext)
    attended_low = attended.reshape(token_rows, model_width)

    out_t = packed_all[:, :model_width]
    layer_input = characters.astype(jnp.float32).reshape(token_rows, model_width)
    middle = layer_input + nt(attended_low, out_t) + out_bias
    normed_two_low = low(normalize(middle, gain_two, bias_two))
    upstream = cotangent.reshape(token_rows, model_width)
    gated_low, expanded_grad, expand_sums, forward, normed_two_grad = run_gate(
        normed_two_low, upstream, packed_all, expand_bias
    )
    layer_output = low(middle + forward + shrink_bias).reshape(characters.shape)

    bits = dp_bits()
    grid_dims = (2,) * (2 + bits)
    link_dims = ["x", "c"] + list(range(bits - 1, -1, -1))

    def hidden_sum(left_rows, right_rows):
        sums = low(across(left_rows, right_rows))
        return Halving(
            sums.reshape((groups,) + grid_dims + (block, model_width)), [None] + link_dims
        )

    shrink_sum = hidden_sum(gated_low, upstream)
    shrink_sum.start("c")
    expand_sum = hidden_sum(expanded_grad, normed_two_low)
    expand_sum.start("c")
    shrink_sum.finish()
    expand_sum.finish()
    marks = [mark(shrink_sum.blocks), mark(expand_sum.blocks)]

    upstream_float = upstream.astype(jnp.float32)
    grad_shrink_bias = jnp.sum(upstream_float, axis=0)
    grad_expand_bias = (
        jnp.sum(expand_sums[:, 0], axis=0)
        .reshape(groups, owners, block)
        .transpose(1, 0, 2)
        .reshape(groups, model_width)
    )

    unused_norm, norm_two_back = jax.vjp(normalize, middle, gain_two, bias_two)
    middle_part, grad_gain_two, grad_bias_two = norm_two_back(normed_two_grad)
    middle_grad = upstream_float + middle_part
    branch_grad = low(middle_grad)
    grad_out_bias = jnp.sum(branch_grad.astype(jnp.float32), axis=0)
    grad_out = low(across(attended_low, branch_grad))
    attended_grad = low(nn(branch_grad, out_t)).reshape(characters.shape)
    pairs = model_width // PAIR
    early = 2 * pairs // 3
    kept = run_backward(
        (0, early), lengths, base, query_low, key_ext, value_ext, attended_grad, totals, (), marks
    )
    marks = one_round(shrink_sum, expand_sum, 0) + [mark(root_all)]
    kept = run_backward(
        (early, pairs - early),
        lengths,
        base,
        query_low,
        key_ext,
        value_ext,
        attended_grad,
        totals,
        kept,
        marks,
    )
    query_grad, key_grad, value_grad = kept
    marks = one_round(shrink_sum, expand_sum, 1)

    pair_grad = jnp.stack([key_grad, value_grad])
    from_above = lax.ppermute(
        pair_grad[:, :, :WIN], "seq", [(i + 1, i) for i in range(ends)]
    )
    from_below = lax.ppermute(
        pair_grad[:, :, block_size + WIN :], "seq", [(i, i + 1) for i in range(ends)]
    )
    from_above = after(from_above, *marks)
    pair_own = pair_grad[:, :, WIN : WIN + block_size]
    pair_low = jnp.concatenate(
        [
            add_low(pair_own[:, :, :WIN], from_below),
            pair_own[:, :, WIN : block_size - WIN],
            add_low(pair_own[:, :, block_size - WIN :], from_above),
        ],
        axis=2,
    ).reshape(2, token_rows, model_width)
    query_rows = query_grad.reshape(token_rows, model_width)
    for i in range(2, len(rounds())):
        marks = one_round(shrink_sum, expand_sum, i)
    shrink_own, expand_own = shrink_sum.blocks, expand_sum.blocks
    hidden_own = jnp.stack(
        [low(own).reshape(hidden_block, model_width) for own in (shrink_own, expand_own)]
    )

    grads = jnp.stack(
        [
            low(across(normed_low, query_rows)),
            low(across(normed_low, pair_low[0])),
            low(across(normed_low, pair_low[1])),
            grad_out,
        ]
    ).reshape((2, 2) + (2, seq_count // 2) + (2,) * bits + (block, model_width))
    core_sum = Halving(grads, ["x", "c"])
    core_sum.start("c")
    core_sum.finish()
    halves = [
        Halving(core_sum.blocks[:, i], ["x", None] + list(range(bits - 1, -1, -1)))
        for i in range(2)
    ]
    for i in range(len(rounds())):
        one_round(*halves, i, jnp.stack(marks) if i == 0 else None)
    attend_own = jnp.concatenate([half.blocks for half in halves])
    grad_query_bias = jnp.sum(query_rows.astype(jnp.float32), axis=0)
    grad_value_bias = jnp.sum(pair_low[1].astype(jnp.float32), axis=0)
    normed_grad = (
        nn(query_rows, qkv_t[:model_width])
        + nn(pair_low[0], qkv_t[model_width : 2 * model_width])
        + nn(pair_low[1], qkv_t[2 * model_width :])
    )
    unused_first, norm_one_back = jax.vjp(normalize, layer_input, gain_one, bias_one)
    input_part, grad_gain_one, grad_bias_one = norm_one_back(normed_grad)
    characters_grad = low(middle_grad + input_part).reshape(characters.shape)
    vector_terms = jnp.concatenate(
        [
            jnp.stack(
                [
                    grad_gain_one,
                    grad_bias_one,
                    grad_query_bias,
                    grad_value_bias,
                    grad_out_bias,
                    grad_gain_two,
                    grad_bias_two,
                    grad_shrink_bias,
                ]
            ),
            grad_expand_bias.reshape(-1, model_width),
        ],
        axis=0,
    )
    whole = spread(low(attend_own)).transpose(1, 0, 2, 3).reshape(model_width, model_width)
    token = attend_own[0, 0, :128]
    vector_terms = after(vector_terms, token)
    vector_some = jnp.sum(spread(vector_terms), axis=0)

    expand_rc = roots[:, :hidden_block].reshape(seq_count * hidden_block, part)
    attend_rc = roots[:, hidden_block : hidden_block + block].reshape(rows_own, model_width)
    shrink_rc = roots[:, hidden_block + block : cut].reshape(rows_own, model_width)
    shrink_lw = root_all[:, :, :hidden_block].reshape(seq_count, part, part)
    attend_lw = root_all[:, :, hidden_block : hidden_block + block].reshape(
        model_width, model_width
    )
    expand_lw = root_all[:, :, hidden_block + block :].reshape(model_width, model_width)

    panels = lax.all_gather(hidden_own, "dp", axis=1, tiled=True)
    row_sets = spread(hidden_own, "seq")
    index = dp_index.astype(jnp.int32)
    products, turns = run_hidden(
        seq_count,
        block,
        dp_count,
        index,
        panels,
        row_sets,
        expand_rc,
        shrink_rc,
        expand_lw,
        shrink_lw,
        token,
    )
    back = swap(products)
    turned_back = swap(turns)
    to_return = run_attend(
        seq_count,
        block,
        dp_count,
        index,
        grad_scale,
        whole,
        attend_own.reshape(rows_own, model_width),
        attend_rc,
        attend_lw,
        products[0, 0, :128],
    )
    returned = swap(to_return)[:, :, :block].astype(jnp.float32)
    vector_some = after(vector_some, returned[0, 0, 0, :128])
    vector_sum = jnp.sum(spread(vector_some, "seq"), axis=0)
    vector_grad = vector_sum * grad_scale
    vector_newacc = vector_acc + vector_grad * vector_grad
    vector_new = vectors - VECTOR_RATE * vector_grad / (jnp.sqrt(vector_newacc) + 1e-08)

    few = block + -block % 16
    much = hidden_block + -hidden_block % 16
    starts = [0, much, 2 * much, 3 * much, 3 * much + few, 3 * much + 2 * few, 3 * much + 3 * few]
    sizes = [hidden_block] * 3 + [block] * 3 + [16]
    parts = [back[:, i : i + n] for i, n in zip(starts, sizes)]

    def unfold(blocks):
        return blocks.transpose(1, 0, 2).reshape(blocks.shape[1], -1)

    def total(blocks):
        return jnp.sum(blocks.astype(jnp.float32), axis=0)

    totals_all = jnp.sum(total(parts[6])[:6, 0].reshape(2, 3), axis=1)
    squares = totals_all * square_scale / (model_width * hidden) + STAT_EPSILON
    shrink_scale = square_scale / squares[0]
    expand_scale = square_scale / squares[1]
    shrink_newleft = 0.5 * shrink_left + unfold(parts[0]).astype(jnp.float32) * (
        0.5 * shrink_scale / model_width
    )
    shrink_newright_t = 0.5 * shrink_right.T + total(parts[3]) * (0.5 * shrink_scale / hidden)
    expand_newright_t = 0.5 * expand_right.T + unfold(parts[1]).astype(jnp.float32) * (
        0.5 * expand_scale / model_width
    )
    expand_newleft = 0.5 * expand_left + total(parts[4]) * (0.5 * expand_scale / hidden)
    expand_rows = unfold(parts[5]).astype(jnp.float32) * grad_scale
    expand_direction_t = total(parts[2]) * (grad_scale * lax.rsqrt(squares[1]))
    shrink_direction_t = unfold(total(turned_back)[:, :block]) * (
        grad_scale * lax.rsqrt(squares[0])
    )
    expand_newmoment_t, expand_newweight_t = finish(
        expand_direction_t, expand_moment.T, expand_t, model_width
    )
    shrink_newmoment_t, shrink_newweight_t = finish(
        shrink_direction_t, shrink_moment.T, shrink_t, hidden
    )
    shrink_grad = shrink_own.reshape(hidden_block, model_width) * grad_scale

    attend_newleft = 0.5 * attend_left + returned[:, 0].transpose(1, 0, 2)
    attend_newright_t = 0.5 * attend_right.transpose(1, 2, 0) + returned[:, 1]
    attend_rows = returned[:, 3].transpose(1, 0, 2) * grad_scale
    attend_newmoment_t, attend_newweight_t = finish(
        returned[:, 2], attend_moment.transpose(1, 2, 0), attend_t, model_width
    )
    return (
        layer_output,
        characters_grad,
        attend_rows,
        attend_newmoment_t.transpose(2, 0, 1),
        attend_newweight_t.transpose(2, 0, 1),
        attend_newleft,
        attend_newright_t.transpose(2, 0, 1),
        expand_rows,
        expand_newmoment_t.T,
        expand_newweight_t.T,
        expand_newleft,
        expand_newright_t.T,
        shrink_grad,
        shrink_newmoment_t.T,
        shrink_newweight_t.T,
        shrink_newleft,
        shrink_newright_t.T,
        vector_grad,
        vector_newacc,
        vector_new,
    )


def solution(mesh):
    return jax.shard_map(
        shards,
        mesh=mesh,
        in_specs=(
            P("dp", "seq", None),
            P("dp", "seq", None),
            P("dp"),
            P(),
            P(),
            P(None, None, ("seq", "dp")),
            P(None, None, ("seq", "dp")),
            P(("seq", "dp"), None, None),
            P(None, None, ("seq", "dp")),
            P(("seq", "dp"), None, None),
            P(None, None, ("seq", "dp")),
            P(None, ("seq", "dp")),
            P(None, ("seq", "dp")),
            P(("seq", "dp"), None),
            P(None, ("seq", "dp")),
            P(("seq", "dp"), None),
            P(None, ("seq", "dp")),
            P(None, ("seq", "dp")),
            P(None, ("seq", "dp")),
            P(("seq", "dp"), None),
            P(None, ("seq", "dp")),
            P(("seq", "dp"), None),
            P(None, ("seq", "dp")),
        ),
        out_specs=(
            P("dp", "seq", None),
            P("dp", "seq", None),
            P(("seq", "dp"), None, None),
            P(None, None, ("seq", "dp")),
            P(None, None, ("seq", "dp")),
            P(("seq", "dp"), None, None),
            P(None, None, ("seq", "dp")),
            P(("seq", "dp"), None),
            P(None, ("seq", "dp")),
            P(None, ("seq", "dp")),
            P(("seq", "dp"), None),
            P(None, ("seq", "dp")),
            P(("seq", "dp"), None),
            P(None, ("seq", "dp")),
            P(None, ("seq", "dp")),
            P(("seq", "dp"), None),
            P(None, ("seq", "dp")),
            P(),
            P(),
            P(),
        ),
        check_vma=False,
    )
```

```python
import functools
import math

import jax
import jax.numpy as jnp
from jax import lax
from jax.experimental import pallas as pl
from jax.experimental.pallas import tpu as pltpu
from jax.sharding import PartitionSpec as P

HEAD = 64
WIN = 128
PAIR = 2 * HEAD
KEYS = 3 * WIN
VMEM_BYTES = 56 * 1024 * 1024

EPSILON = 1e-05
STAT_EPSILON = 1e-06
MATRIX_RATE = 0.5
VECTOR_RATE = 0.3
MOMENTUM = 0.9
MASKED = -1e30

PHI_POLY = (
    0.7978849414608439,
    0.03633308457157131,
    -3.259497261642231e-05,
    -5.530619510506789e-05,
    3.964744703196676e-06,
    -1.3226336477723372e-07,
    1.7561715138424972e-09,
)


def nt(left_rows, right_rows):
    return lax.dot_general(
        left_rows, right_rows, (((1,), (1,)), ((), ())), preferred_element_type=jnp.float32
    )


def nn(left_rows, right_cols):
    return jnp.dot(left_rows, right_cols, preferred_element_type=jnp.float32)


def across(left_rows, right_rows):
    return lax.dot_general(
        left_rows, right_rows, (((0,), (0,)), ((), ())), preferred_element_type=jnp.float32
    )


def low(values):
    return values.astype(jnp.bfloat16)


def normalize(values, gain_row, bias_row):
    centre = values - jnp.mean(values, axis=-1, keepdims=True)
    spread = jnp.mean(centre * centre, axis=-1, keepdims=True)
    return centre * lax.rsqrt(spread + EPSILON) * gain_row + bias_row


def params():
    return pltpu.CompilerParams(vmem_limit_bytes=VMEM_BYTES)


def write_mask(bias_ref, length, base, blocks):
    for i in range(blocks):
        key = lax.broadcasted_iota(jnp.int32, (KEYS, WIN), 0)
        query = lax.broadcasted_iota(jnp.int32, (KEYS, WIN), 1)
        place = key + (base + (i - 1) * WIN)
        near = (key >= query) & (key <= query + 2 * WIN)
        seen = ((place >= 0) & (place < length)) | (key == query + WIN)
        bias_ref[i] = jnp.where(near & seen, 0.0, MASKED)


def stacked(rows, scale):
    lane = lax.broadcasted_iota(jnp.int32, rows.shape, 1)
    rows = rows.astype(jnp.float32) * scale
    first = jnp.where(lane < HEAD, rows, 0.0)
    second = jnp.where(lane < HEAD, 0.0, rows)
    return low(jnp.concatenate([first, second], axis=0))


def unstacked(turned):
    pair = jnp.concatenate([turned[:HEAD, :WIN], turned[HEAD:, WIN:]], axis=0)
    return pair.T


def attend_forward(blocks, lengths, base, q_ref, k_ref, v_ref, o_ref, total_ref, bias_ref):
    text = pl.program_id(0)

    @pl.when(pl.program_id(1) == 0)
    def _():
        write_mask(bias_ref, lengths[text], base[0], blocks)

    def window(ref, i):
        return ref[0, i * WIN : i * WIN + KEYS, :]

    def own(i):
        return slice(i * WIN, (i + 1) * WIN)

    every = range(blocks)
    scores = [nt(window(k_ref, i), stacked(q_ref[0, own(i), :], 0.125)) for i in every]
    weights = []
    totals = []
    for i in every:
        bias = bias_ref[i]
        masked = scores[i] + jnp.concatenate([bias, bias], axis=1)
        peak = jnp.max(masked, axis=0, keepdims=True)
        weight = jnp.exp(masked - peak)
        total = jnp.sum(weight, axis=0, keepdims=True)
        weights.append(low(weight))
        totals.append(1.0 / total)
        log_total = peak + jnp.log(total)
        total_ref[0, 0, 2 * i : 2 * i + 1, :] = log_total[:, :WIN]
        total_ref[0, 0, 2 * i + 1 : 2 * i + 2, :] = log_total[:, WIN:]
    mixed = [across(window(v_ref, i), weights[i]) for i in every]
    for i in every:
        o_ref[0, own(i), :] = low(unstacked(mixed[i] * totals[i]))


def attend_backward(
    blocks,
    extra,
    lengths,
    base,
    q_ref,
    k_ref,
    v_ref,
    up_ref,
    total_ref,
    *rest,
):
    dq_ref, dk_ref, dv_ref, bias_ref, dk_sum, dv_sum = rest[extra:]
    text = pl.program_id(0)

    @pl.when(pl.program_id(1) == 0)
    def _():
        write_mask(bias_ref, lengths[text], base[0], blocks)

    def window(i):
        return slice(i * WIN, i * WIN + KEYS)

    def own(i):
        return slice(i * WIN, (i + 1) * WIN)

    every = range(blocks)
    queries = [stacked(q_ref[0, own(i), :], 0.125) for i in every]
    upstream = [stacked(up_ref[0, own(i), :], 1.0) for i in every]
    scores = [nt(k_ref[0, window(i), :], queries[i]) for i in every]
    weight_grads = [nt(v_ref[0, window(i), :], upstream[i]) for i in every]
    weights = []
    score_grads = []
    for i in every:
        bias = bias_ref[i]
        log_total = jnp.concatenate(
            [total_ref[0, 0, 2 * i : 2 * i + 1, :], total_ref[0, 0, 2 * i + 1 : 2 * i + 2, :]],
            axis=1,
        )
        weight = jnp.exp(scores[i] + jnp.concatenate([bias, bias], axis=1) - log_total)
        product = weight * weight_grads[i]
        score_grads.append(
            low(product - weight * jnp.sum(product, axis=0, keepdims=True))
        )
        weights.append(low(weight))
    dk_sum[...] = jnp.zeros_like(dk_sum)
    dv_sum[...] = jnp.zeros_like(dv_sum)
    for i in every:
        dv_sum[window(i), :] += nn(weights[i], upstream[i])
        dk_sum[window(i), :] += nn(score_grads[i], queries[i])
    turned = [across(k_ref[0, window(i), :], score_grads[i]) for i in every]
    for i in every:
        dq_ref[0, own(i), :] = low(unstacked(turned[i]) * 0.125)
    dk_ref[0] = low(dk_sum[...])
    dv_ref[0] = low(dv_sum[...])


def attention_specs(block_size):
    wide = block_size + 2 * WIN
    blocks = block_size // WIN
    own = pl.BlockSpec((1, block_size, PAIR), lambda t, g: (t, 0, g))
    ext = pl.BlockSpec((1, wide, PAIR), lambda t, g: (t, 0, g))
    sums = pl.BlockSpec((1, 1, 2 * blocks, WIN), lambda t, g: (t, g, 0, 0))
    smem = pl.BlockSpec(memory_space=pltpu.SMEM)
    return wide, blocks, own, ext, sums, smem


def run_forward(lengths, base, query, key_ext, value_ext):
    texts, block_size, width = query.shape
    wide, blocks, own, ext, sums, smem = attention_specs(block_size)
    work = texts * blocks * (width // PAIR)
    return pl.pallas_call(
        functools.partial(attend_forward, blocks),
        grid=(texts, width // PAIR),
        in_specs=[smem, smem, own, ext, ext],
        out_specs=[own, sums],
        out_shape=[
            jax.ShapeDtypeStruct(query.shape, jnp.bfloat16),
            jax.ShapeDtypeStruct((texts, width // PAIR, 2 * blocks, WIN), jnp.float32),
        ],
        scratch_shapes=[pltpu.VMEM((blocks, KEYS, WIN), jnp.float32)],
        compiler_params=params(),
        cost_estimate=pl.CostEstimate(
            flops=work * 4 * KEYS * PAIR * 2 * WIN,
            bytes_accessed=query.size * 2 * 5,
            transcendentals=work * KEYS * 2 * WIN,
        ),
        name="attend_forward",
    )(lengths, base, query, key_ext, value_ext)


def run_backward(pairs, lengths, base, query, key_ext, value_ext, upstream, totals, kept, first):
    texts, block_size, width = query.shape
    wide = block_size + 2 * WIN
    blocks = block_size // WIN
    low_pair, count = pairs
    own = pl.BlockSpec((1, block_size, PAIR), lambda t, g: (t, 0, low_pair + g))
    ext = pl.BlockSpec((1, wide, PAIR), lambda t, g: (t, 0, low_pair + g))
    sums = pl.BlockSpec((1, 1, 2 * blocks, WIN), lambda t, g: (t, low_pair + g, 0, 0))
    smem = pl.BlockSpec(memory_space=pltpu.SMEM)
    others = tuple(kept) + tuple(first)
    work = texts * blocks * count
    return pl.pallas_call(
        functools.partial(attend_backward, blocks, len(others)),
        grid=(texts, count),
        in_specs=[smem, smem, own, ext, ext, own, sums]
        + [pl.BlockSpec(memory_space=pl.ANY)] * len(others),
        out_specs=[own, ext, ext],
        out_shape=[
            jax.ShapeDtypeStruct(query.shape, jnp.bfloat16),
            jax.ShapeDtypeStruct(key_ext.shape, jnp.bfloat16),
            jax.ShapeDtypeStruct(key_ext.shape, jnp.bfloat16),
        ],
        scratch_shapes=[
            pltpu.VMEM((blocks, KEYS, WIN), jnp.float32),
            pltpu.VMEM((wide, PAIR), jnp.float32),
            pltpu.VMEM((wide, PAIR), jnp.float32),
        ],
        input_output_aliases={7 + i: i for i in range(len(kept))},
        compiler_params=params(),
        cost_estimate=pl.CostEstimate(
            flops=work * 10 * KEYS * PAIR * 2 * WIN,
            bytes_accessed=query.size * 10,
            transcendentals=work * KEYS * 2 * WIN,
        ),
        name="attend_backward",
    )(lengths, base, query, key_ext, value_ext, upstream, totals, *others)


GATE_ROWS = 512
GATE_COLS = 256
GATE_SLAB = 32
BELL = 1.0 / math.sqrt(2.0 * math.pi)


def gate_kernel(
    rows_ref,
    upstream_ref,
    in_ref,
    out_ref,
    bias_ref,
    gate_ref,
    grad_ref,
    sums_ref,
    forward_ref,
    back_ref,
    forward_sum,
    back_sum,
):
    panel, tile = pl.program_id(0), pl.program_id(1)
    part = rows_ref.shape[1]
    ones = jnp.ones((8, GATE_ROWS), jnp.bfloat16)
    chunks = part // GATE_COLS

    def products(c):
        cols = slice(c * GATE_COLS, (c + 1) * GATE_COLS)
        hidden = nt(rows_ref[...], in_ref[cols, :]) + bias_ref[:, cols]
        return hidden, nn(upstream_ref[...], out_ref[:, cols])

    later = products(0)
    for c in range(chunks):
        hidden, hidden_grad = later
        if c + 1 < chunks:
            later = products(c + 1)
        cols = slice(c * GATE_COLS, (c + 1) * GATE_COLS)
        for i in range(GATE_ROWS // GATE_SLAB):
            own = slice(i * GATE_SLAB, (i + 1) * GATE_SLAB)
            u = hidden[own, :]
            square = u * u
            poly = PHI_POLY[-1] * square + PHI_POLY[-2]
            for term in PHI_POLY[-3::-1]:
                poly = poly * square + term
            half = 0.5 * jnp.tanh(poly * u)
            phi = half + 0.5
            bell = jnp.exp2(square * (-0.5 * math.log2(math.e)))
            gate_ref[own, cols] = low(u * phi)
            grad_ref[own, cols] = low(hidden_grad[own, :] * (phi + (u * BELL) * bell))
        sums_ref[0, :, cols] = nn(ones, grad_ref[:, cols])
    slot = pl.ds(pl.multiple_of(tile * GATE_ROWS, GATE_ROWS), GATE_ROWS)
    forward = nt(gate_ref[...], out_ref[...])
    back = nn(grad_ref[...], in_ref[...])

    @pl.when(panel == 0)
    def _():
        forward_sum[slot, :] = forward
        back_sum[slot, :] = back

    @pl.when(panel > 0)
    def _():
        forward_sum[slot, :] += forward
        back_sum[slot, :] += back

    @pl.when(panel == pl.num_programs(0) - 1)
    def _():
        forward_ref[...] = forward_sum[slot, :]
        back_ref[...] = back_sum[slot, :]


def run_gate(rows, upstream, packed, bias):
    tokens, width = rows.shape
    hidden = bias.shape[1]
    groups = hidden // width
    tiles = tokens // GATE_ROWS
    row_spec = pl.BlockSpec((GATE_ROWS, width), lambda j, i: (i, 0))
    out_spec = pl.BlockSpec((GATE_ROWS, width), lambda j, i: (i, j))
    last_spec = pl.BlockSpec(
        (GATE_ROWS, width), lambda j, i: (jnp.where(j == groups - 1, i, 0), 0)
    )
    wide_out = jax.ShapeDtypeStruct((tokens, hidden), jnp.bfloat16)
    row_out = jax.ShapeDtypeStruct((tokens, width), jnp.float32)
    return pl.pallas_call(
        gate_kernel,
        grid=(groups, tiles),
        in_specs=[
            row_spec,
            row_spec,
            pl.BlockSpec((width, width), lambda j, i: (0, 1 + groups + j)),
            pl.BlockSpec((width, width), lambda j, i: (0, 1 + j)),
            pl.BlockSpec((1, width), lambda j, i: (0, j)),
        ],
        out_specs=[
            out_spec,
            out_spec,
            pl.BlockSpec((1, 8, width), lambda j, i: (i, 0, j)),
            last_spec,
            last_spec,
        ],
        out_shape=[
            wide_out,
            wide_out,
            jax.ShapeDtypeStruct((tiles, 8, hidden), jnp.float32),
            row_out,
            row_out,
        ],
        scratch_shapes=[pltpu.VMEM((tokens, width), jnp.float32)] * 2,
        compiler_params=params(),
        cost_estimate=pl.CostEstimate(
            flops=tokens * width * hidden,
            bytes_accessed=4 * (tokens * width + width * hidden + tokens * hidden),
            transcendentals=2 * tokens * hidden,
        ),
        name="gate",
    )(rows, upstream, packed, packed, bias)


def flip(blocks, axis, mask):
    count = lax.axis_size(axis)
    return lax.ppermute(blocks, axis, [(i, i ^ mask) for i in range(count)])


def swap(blocks):
    return lax.all_to_all(blocks, "seq", split_axis=0, concat_axis=0, tiled=True)


def spread(block, axis="dp"):
    copies = jnp.broadcast_to(block[None], (lax.axis_size(axis),) + block.shape)
    return lax.all_to_all(copies, axis, split_axis=0, concat_axis=0, tiled=True)


def ordered(bit, own, other, dim):
    return jnp.where(
        bit == 0, jnp.stack([own, other], axis=dim), jnp.stack([other, own], axis=dim)
    )


def after(value, *first):
    return lax.optimization_barrier((value,) + first)[0]


def add_low(left, right):
    return low(left.astype(jnp.float32) + right.astype(jnp.float32))


def dp_bits():
    return lax.axis_size("dp").bit_length() - 1


class Halving:
    def __init__(self, blocks, dims):
        self.blocks, self.dims = blocks, list(dims)

    def start(self, dim):
        place = self.dims.index(dim)
        axis, shift = ("seq", "cx".index(dim)) if isinstance(dim, str) else ("dp", dim)
        bit = lax.axis_index(axis) // (1 << shift) % 2
        sent = lax.dynamic_index_in_dim(self.blocks, 1 - bit, place, keepdims=False)
        self.kept = lax.dynamic_index_in_dim(self.blocks, bit, place, keepdims=False)
        self.got = flip(sent, axis, 1 << shift)
        self.dims.pop(place)

    def finish(self, last=False, first=None):
        got = self.got if first is None else after(self.got, first)
        total = self.kept.astype(jnp.float32) + got.astype(jnp.float32)
        self.blocks = total if last else low(total)


def rounds():
    bits = list(range(dp_bits()))
    return list(zip(["x"] + bits, bits + ["x"]))


def one_round(one, other, i, first=None):
    left, right = rounds()[i]
    last = i == len(rounds()) - 1
    one.start(left)
    other.start(right)
    one.finish(last, first)
    other.finish(last, first)
    return [mark(one.blocks), mark(other.blocks)]


def mark(array):
    return array.reshape(-1, array.shape[-1])[:8, :128]


def picker(count, block, dp_count, dp_index, width):
    row = lax.broadcasted_iota(jnp.int32, (count * block, width), 0)
    col = lax.broadcasted_iota(jnp.int32, (count * block, width), 1)
    found = jnp.zeros(row.shape, jnp.float32)
    for s in range(count):
        here = (row >= s * block) & (row < (s + 1) * block)
        place = row + (s * (dp_count - 1) + dp_index) * block
        found = jnp.where(here & (col == place), 1.0, found)
    return low(found)


def padded(rows):
    extra = -rows.shape[0] % 16
    if extra:
        rows = jnp.concatenate([rows, jnp.zeros((extra, rows.shape[1]), jnp.float32)])
    return low(rows)


def hidden_products(
    seq_count, block, dp_count, dp_index, panels, row_sets, expand_rc, expand_lw, shrink_lr, shrink_rt
):
    shrink, expand = panels[0], panels[1]
    width = shrink.shape[0]
    pick = picker(seq_count, block, dp_count, dp_index, width)
    shrink_cols = low(nt(pick, shrink))
    expand_cols = nt(pick, expand)
    turned = low(nt(shrink_rt, low(nn(shrink_lr, shrink))))
    shrink_right = nn(shrink_cols, shrink)
    expand_left = nn(low(expand_cols), expand)
    expand_turned = nt(low(nn(expand_rc, expand)), expand_lw)
    owned = expand_rc.shape[0] // seq_count
    sums = [
        jnp.sum(jnp.sum(jnp.square(p.astype(jnp.float32)), axis=0, keepdims=True), axis=1, keepdims=True)
        for p in (shrink, expand)
    ]
    line = lax.broadcasted_iota(jnp.int32, (16, width), 0)
    marks = jnp.zeros((16, width), jnp.float32)
    for i, value in enumerate(sums):
        for j in range(3):
            piece = low(jnp.broadcast_to(value, (16, width))).astype(jnp.float32)
            marks = jnp.where(line == 3 * i + j, piece, marks)
            value = value - piece[:1, :1]
    pieces = []
    for s in range(seq_count):
        rows = slice(s * owned, (s + 1) * owned)
        few = slice(s * block, (s + 1) * block)
        pieces.append(
            [
                padded(nt(row_sets[s, 0], shrink)),
                padded(nt(row_sets[s, 1], expand)),
                padded(expand_turned[rows]),
                padded(shrink_right[few]),
                padded(expand_left[few]),
                padded(expand_cols[few]),
                low(marks),
            ]
        )
    return pieces, turned


def hidden_kernel(
    seq_count,
    block,
    dp_count,
    index_ref,
    panels_ref,
    rows_ref,
    expand_rc_ref,
    expand_lw_ref,
    shrink_lr_ref,
    shrink_rt_ref,
    token_ref,
    out_ref,
    turn_ref,
):
    pieces, turned = hidden_products(
        seq_count,
        block,
        dp_count,
        index_ref[0],
        panels_ref,
        rows_ref,
        expand_rc_ref[...],
        expand_lw_ref[...],
        shrink_lr_ref[...],
        shrink_rt_ref[...],
    )
    turn_ref[...] = turned
    for s in range(seq_count):
        start = 0
        for piece in pieces[s]:
            out_ref[s, start : start + piece.shape[0], :] = piece
            start += piece.shape[0]


def run_hidden(seq_count, block, dp_count, dp_index, panels, row_sets, rc, lw, lr, rt, token):
    width = panels.shape[1]
    owned = rc.shape[0] // seq_count
    if owned % 16 or block % 8:
        pieces, turned = hidden_products(
            seq_count, block, dp_count, dp_index, panels, row_sets, rc, lw, lr, rt
        )
        return jnp.stack([jnp.concatenate(piece) for piece in pieces]), turned
    few = block + -block % 16
    rows_out = 3 * owned + 3 * few + 16
    vmem = pl.BlockSpec(memory_space=pltpu.VMEM)
    return pl.pallas_call(
        functools.partial(hidden_kernel, seq_count, block, dp_count),
        in_specs=[pl.BlockSpec(memory_space=pltpu.SMEM)]
        + [vmem] * 6
        + [pl.BlockSpec(memory_space=pl.ANY)],
        out_specs=[vmem, vmem],
        out_shape=[
            jax.ShapeDtypeStruct((seq_count, rows_out, width), jnp.bfloat16),
            jax.ShapeDtypeStruct((width, seq_count * owned), jnp.bfloat16),
        ],
        compiler_params=params(),
        cost_estimate=pl.CostEstimate(
            flops=40 * owned * width * width, bytes_accessed=12 * width * width, transcendentals=0
        ),
        name="hidden_update",
    )(dp_index.reshape(1), panels, row_sets, rc, lw, lr, rt, token)


def halves_of(values, keep=lambda high: high):
    extra = 16 - values.shape[0]
    if extra:
        values = jnp.concatenate([values, jnp.zeros((extra, values.shape[1]), jnp.float32)])
    high = keep(low(values))
    return jnp.concatenate([high, low(values - high.astype(jnp.float32))])


def from_halves(parts):
    total = jnp.sum(parts.astype(jnp.float32), axis=0)
    return total[:16] + total[16:]


def attend_products(seq_count, block, dp_count, dp_index, scale, whole, own, rc, lw):
    width = whole.shape[0]
    pick = picker(seq_count, block, dp_count, dp_index, width)
    wide = whole.astype(jnp.float32)
    total = jnp.sum(jnp.sum(wide * wide, axis=0, keepdims=True), axis=1, keepdims=True)
    square = total * (scale * scale / (width * width)) + STAT_EPSILON
    gram = (0.5 * scale * scale / width) / square
    left = nt(low(own), whole) * gram
    right = nn(low(nt(pick, whole)), whole) * gram
    turned = nt(low(nt(rc, whole)), lw) * (scale * lax.rsqrt(square))
    return [
        [padded(piece[s * block : (s + 1) * block]) for piece in (left, right, turned, own)]
        for s in range(seq_count)
    ]


def attend_kernel(
    seq_count,
    block,
    dp_count,
    scale,
    index_ref,
    whole_ref,
    own_ref,
    rc_ref,
    lw_ref,
    vector_ref,
    token_ref,
    out_ref,
):
    vectors = halves_of(from_halves(vector_ref[...]))
    pieces = attend_products(
        seq_count,
        block,
        dp_count,
        index_ref[0],
        scale,
        whole_ref[...],
        own_ref[...],
        rc_ref[...],
        lw_ref[...],
    )
    for s in range(seq_count):
        for i, piece in enumerate(pieces[s]):
            out_ref[s, i] = piece
        out_ref[s, len(pieces[s])] = vectors


def run_attend(seq_count, block, dp_count, dp_index, scale, whole, own, rc, lw, vectors, token):
    width = whole.shape[0]
    few = block + -block % 16
    if few != 32 or block % 8:
        pieces = attend_products(
            seq_count, block, dp_count, dp_index, scale, whole, own, rc, lw
        )
        sums = halves_of(from_halves(vectors), lax.optimization_barrier)
        fill = ((0, 32 - few), (0, 0))
        return jnp.stack(
            [jnp.stack([jnp.pad(p, fill) for p in piece] + [sums]) for piece in pieces]
        )
    vmem = pl.BlockSpec(memory_space=pltpu.VMEM)
    return pl.pallas_call(
        functools.partial(attend_kernel, seq_count, block, dp_count, scale),
        in_specs=[pl.BlockSpec(memory_space=pltpu.SMEM)]
        + [vmem] * 5
        + [pl.BlockSpec(memory_space=pl.ANY)],
        out_specs=vmem,
        out_shape=jax.ShapeDtypeStruct((seq_count, 5, few, width), jnp.bfloat16),
        compiler_params=params(),
        cost_estimate=pl.CostEstimate(
            flops=10 * own.shape[0] * width * width, bytes_accessed=6 * width * width, transcendentals=0
        ),
        name="attend_update",
    )(dp_index.reshape(1), whole, own, rc, lw, vectors, token)


def finish(direction, moment, weight, row_count):
    new_moment = MOMENTUM * moment + direction
    new_weight = weight - MATRIX_RATE / math.sqrt(row_count) * new_moment
    return (new_moment, new_weight)


def shards(
    characters,
    cotangent,
    lengths,
    vectors,
    vector_acc,
    attend_weight,
    attend_moment,
    attend_left,
    attend_right,
    attend_rootleft,
    attend_rootright,
    expand_weight,
    expand_moment,
    expand_left,
    expand_right,
    expand_rootleft,
    expand_rootright,
    shrink_weight,
    shrink_moment,
    shrink_left,
    shrink_right,
    shrink_rootleft,
    shrink_rootright,
):
    text_count, block_size, model_width = characters.shape
    token_rows = text_count * block_size
    both = ("seq", "dp")
    seq_count = lax.axis_size("seq")
    dp_count = lax.axis_size("dp")
    seq_index = lax.axis_index("seq")
    dp_index = lax.axis_index("dp")
    core = seq_index % 2
    chip = seq_index // 2
    tokens_all = token_rows * seq_count * dp_count
    grad_scale = 1.0 / math.sqrt(tokens_all)
    square_scale = grad_scale * grad_scale
    hidden = expand_weight.shape[1] * seq_count * dp_count
    part = hidden // seq_count
    block = model_width // (seq_count * dp_count)
    hidden_block = hidden // (seq_count * dp_count)
    rows_own = seq_count * block

    owners = seq_count * dp_count
    groups = hidden // model_width
    ends = seq_count - 1
    before = lax.ppermute(
        characters[:, block_size - WIN :], "seq", [(i, i + 1) for i in range(ends)]
    )
    follow = lax.ppermute(characters[:, :WIN], "seq", [(i + 1, i) for i in range(ends)])

    attend_t = attend_weight.transpose(1, 2, 0)
    expand_t = expand_weight.T
    shrink_t = shrink_weight.T
    packed = jnp.concatenate(
        [
            low(attend_t[3]),
            low(shrink_t)
            .reshape(block, owners, groups, block)
            .transpose(0, 2, 1, 3)
            .reshape(block, hidden),
            low(expand_t)
            .reshape(groups, block, model_width)
            .transpose(1, 0, 2)
            .reshape(block, hidden),
        ],
        axis=1,
    )
    packed_all = lax.all_gather(packed, both, axis=0, tiled=True)
    over_dp = spread(low(attend_t[:3])).transpose(1, 0, 2, 3)

    def panels_of(rows):
        return low(rows).reshape(rows.shape[0], seq_count, part).transpose(1, 0, 2)

    def copies_of(rows):
        return jnp.broadcast_to(low(rows)[None], (seq_count,) + rows.shape)

    root_parts = jnp.concatenate(
        [
            panels_of(expand_rootright.T),
            low(attend_rootright.transpose(1, 2, 0)),
            panels_of(shrink_rootleft),
            low(attend_rootleft).transpose(1, 0, 2),
            copies_of(expand_rootleft),
            copies_of(shrink_rootright.T),
        ],
        axis=1,
    )
    over_chip = ordered(chip, over_dp, flip(over_dp, "seq", 2), 1)

    input_ext = jnp.concatenate([before, characters, follow], axis=1)
    wide = block_size + 2 * WIN

    gain_one = vectors[0]
    bias_one = vectors[1]
    query_bias = vectors[2]
    value_bias = vectors[3]
    out_bias = vectors[4]
    gain_two = vectors[5]
    bias_two = vectors[6]
    shrink_bias = vectors[7]
    expand_bias = vectors[8:].reshape(owners, groups, block).transpose(1, 0, 2).reshape(1, -1)
    normed_ext = low(normalize(input_ext.astype(jnp.float32), gain_one, bias_one))
    over_chip, normed_ext = lax.optimization_barrier((over_chip, normed_ext))
    over_core = ordered(core, over_chip, flip(over_chip, "seq", 1), 2)
    qkv_t = over_core.reshape(3 * model_width, model_width)
    normed_low = normed_ext[:, WIN : WIN + block_size].reshape(token_rows, model_width)
    ext_rows = normed_ext.reshape(text_count * wide, model_width)
    query_low = low(nt(normed_low, qkv_t[:model_width]) + query_bias).reshape(characters.shape)
    key_ext = low(nt(ext_rows, qkv_t[model_width : 2 * model_width])).reshape(
        text_count, wide, model_width
    )
    value_ext = low(nt(ext_rows, qkv_t[2 * model_width :]) + value_bias).reshape(
        text_count, wide, model_width
    )
    roots = swap(after(root_parts, mark(query_low)))
    base = (seq_index * block_size).astype(jnp.int32).reshape(1)
    attended, totals = run_forward(lengths, base, query_low, key_ext, value_ext)
    attended_low = attended.reshape(token_rows, model_width)

    out_t = packed_all[:, :model_width]
    layer_input = characters.astype(jnp.float32).reshape(token_rows, model_width)
    middle = layer_input + nt(attended_low, out_t) + out_bias
    normed_two_low = low(normalize(middle, gain_two, bias_two))
    normed_two_low, roots = lax.optimization_barrier((normed_two_low, roots))
    cut = 2 * hidden_block + block
    root_all = lax.all_gather(roots[:, cut:], "dp", axis=1)
    upstream = cotangent.reshape(token_rows, model_width)
    gated_low, expanded_grad, expand_sums, forward, normed_two_grad = run_gate(
        normed_two_low, upstream, packed_all, expand_bias
    )
    layer_output = low(middle + forward + shrink_bias).reshape(characters.shape)

    bits = dp_bits()
    grid_dims = (2,) * (2 + bits)
    link_dims = ["x", "c"] + list(range(bits - 1, -1, -1))

    def hidden_sum(left_rows, right_rows):
        sums = low(across(left_rows, right_rows))
        return Halving(
            sums.reshape((groups,) + grid_dims + (block, model_width)), [None] + link_dims
        )

    shrink_sum = hidden_sum(gated_low, upstream)
    shrink_sum.start("c")
    expand_sum = hidden_sum(expanded_grad, normed_two_low)
    expand_sum.start("c")
    shrink_sum.finish()
    expand_sum.finish()
    marks = [mark(shrink_sum.blocks), mark(expand_sum.blocks)]

    upstream_float = upstream.astype(jnp.float32)
    grad_shrink_bias = jnp.sum(upstream_float, axis=0)
    grad_expand_bias = (
        jnp.sum(expand_sums[:, 0], axis=0)
        .reshape(groups, owners, block)
        .transpose(1, 0, 2)
        .reshape(groups, model_width)
    )

    unused_norm, norm_two_back = jax.vjp(normalize, middle, gain_two, bias_two)
    middle_part, grad_gain_two, grad_bias_two = norm_two_back(normed_two_grad)
    middle_grad = upstream_float + middle_part
    branch_grad = low(middle_grad)
    grad_out_bias = jnp.sum(branch_grad.astype(jnp.float32), axis=0)
    grad_out = low(across(attended_low, branch_grad))
    attended_grad = low(nn(branch_grad, out_t)).reshape(characters.shape)
    pairs = model_width // PAIR
    early = 2 * pairs // 3
    kept = run_backward(
        (0, early), lengths, base, query_low, key_ext, value_ext, attended_grad, totals, (), marks
    )
    marks = one_round(shrink_sum, expand_sum, 0)
    kept = run_backward(
        (early, pairs - early),
        lengths,
        base,
        query_low,
        key_ext,
        value_ext,
        attended_grad,
        totals,
        kept,
        marks,
    )
    query_grad, key_grad, value_grad = kept
    marks = one_round(shrink_sum, expand_sum, 1)

    pair_grad = jnp.stack([key_grad, value_grad])
    from_above = lax.ppermute(
        pair_grad[:, :, :WIN], "seq", [(i + 1, i) for i in range(ends)]
    )
    from_below = lax.ppermute(
        pair_grad[:, :, block_size + WIN :], "seq", [(i, i + 1) for i in range(ends)]
    )
    from_above = after(from_above, mark(root_all), *marks)
    pair_own = pair_grad[:, :, WIN : WIN + block_size]
    pair_low = jnp.concatenate(
        [
            add_low(pair_own[:, :, :WIN], from_below),
            pair_own[:, :, WIN : block_size - WIN],
            add_low(pair_own[:, :, block_size - WIN :], from_above),
        ],
        axis=2,
    ).reshape(2, token_rows, model_width)
    query_rows = query_grad.reshape(token_rows, model_width)
    grads = jnp.stack(
        [
            low(across(normed_low, query_rows)),
            low(across(normed_low, pair_low[0])),
            low(across(normed_low, pair_low[1])),
            grad_out,
        ]
    ).reshape((2, 2) + (2, seq_count // 2) + (2,) * bits + (block, model_width))
    core_sum = Halving(grads, ["x", "c"])
    core_sum.start("c")
    core_sum.finish()
    for i in range(2, len(rounds())):
        marks = one_round(
            shrink_sum, expand_sum, i, mark(core_sum.kept if i == 2 else core_sum.blocks)
        )
    shrink_own, expand_own = shrink_sum.blocks, expand_sum.blocks
    hidden_own = jnp.stack(
        [low(own).reshape(hidden_block, model_width) for own in (shrink_own, expand_own)]
    )

    halves = [
        Halving(core_sum.blocks[:, i], ["x", None] + list(range(bits - 1, -1, -1)))
        for i in range(2)
    ]
    for i in range(len(rounds())):
        one_round(*halves, i, jnp.stack(marks) if i == 0 else None)
    attend_own = jnp.concatenate([half.blocks for half in halves])
    grad_query_bias = jnp.sum(query_rows.astype(jnp.float32), axis=0)
    grad_value_bias = jnp.sum(pair_low[1].astype(jnp.float32), axis=0)
    normed_grad = (
        nn(query_rows, qkv_t[:model_width])
        + nn(pair_low[0], qkv_t[model_width : 2 * model_width])
        + nn(pair_low[1], qkv_t[2 * model_width :])
    )
    unused_first, norm_one_back = jax.vjp(normalize, layer_input, gain_one, bias_one)
    input_part, grad_gain_one, grad_bias_one = norm_one_back(normed_grad)
    characters_grad = low(middle_grad + input_part).reshape(characters.shape)
    vector_terms = jnp.concatenate(
        [
            jnp.stack(
                [
                    grad_gain_one,
                    grad_bias_one,
                    grad_query_bias,
                    grad_value_bias,
                    grad_out_bias,
                    grad_gain_two,
                    grad_bias_two,
                    grad_shrink_bias,
                ]
            ),
            grad_expand_bias.reshape(-1, model_width),
        ],
        axis=0,
    )
    token = attend_own[0, :1, :128] + attend_own[-1, :1, :128]
    attend_all = lax.all_gather(
        jnp.concatenate(
            [
                low(attend_own).reshape(rows_own, model_width),
                halves_of(vector_terms, lax.optimization_barrier),
            ]
        ),
        "dp",
        axis=0,
    )
    whole = (
        attend_all[:, :rows_own]
        .reshape(dp_count, seq_count, block, model_width)
        .transpose(1, 0, 2, 3)
        .reshape(model_width, model_width)
    )

    expand_rc = roots[:, :hidden_block].reshape(seq_count * hidden_block, part)
    attend_rc = roots[:, hidden_block : hidden_block + block].reshape(rows_own, model_width)
    shrink_lr = roots[:, hidden_block + block : cut].reshape(seq_count * hidden_block, part)
    attend_lw = root_all[:, :, :block].reshape(model_width, model_width)
    expand_lw = root_all[:, :, block : 2 * block].reshape(model_width, model_width)
    shrink_rt = root_all[:, :, 2 * block :].transpose(1, 0, 2, 3).reshape(model_width, model_width)

    panels = lax.all_gather(hidden_own, "dp", axis=1, tiled=True)
    row_sets = ordered(chip, hidden_own, flip(hidden_own, "seq", 2), 0)
    row_sets = ordered(core, row_sets, flip(row_sets, "seq", 1), 1)
    row_sets = row_sets.reshape((seq_count,) + hidden_own.shape)
    index = dp_index.astype(jnp.int32)
    products, turned = run_hidden(
        seq_count,
        block,
        dp_count,
        index,
        panels,
        row_sets,
        expand_rc,
        expand_lw,
        shrink_lr,
        shrink_rt,
        token,
    )
    turned = lax.all_to_all(
        turned.reshape(dp_count, rows_own, seq_count * hidden_block),
        "dp",
        split_axis=0,
        concat_axis=0,
        tiled=True,
    )
    pack = model_width // (seq_count * hidden_block)
    turned = (
        turned.reshape(dp_count // pack, pack, seq_count, block, seq_count * hidden_block)
        .transpose(2, 0, 3, 1, 4)
        .reshape(seq_count, hidden_block, model_width)
    )
    to_owners = jnp.concatenate([products, turned], axis=1)
    back = swap(to_owners)
    to_return = run_attend(
        seq_count,
        block,
        dp_count,
        index,
        grad_scale,
        whole,
        attend_own.reshape(rows_own, model_width),
        attend_rc,
        attend_lw,
        attend_all[:, rows_own:],
        mark(to_owners),
    )
    returned = swap(to_return)
    vector_sum = from_halves(returned[:, 4])[: vectors.shape[0]]
    returned = returned[:, :4, :block].astype(jnp.float32)
    vector_grad = vector_sum * grad_scale
    vector_newacc = vector_acc + vector_grad * vector_grad
    vector_new = vectors - VECTOR_RATE * vector_grad / (jnp.sqrt(vector_newacc) + 1e-08)

    few = block + -block % 16
    much = hidden_block + -hidden_block % 16
    starts = [0, much, 2 * much, 3 * much, 3 * much + few, 3 * much + 2 * few, 3 * much + 3 * few]
    sizes = [hidden_block] * 3 + [block] * 3 + [16]
    parts = [back[:, i : i + n] for i, n in zip(starts, sizes)]

    def unfold(blocks):
        return blocks.transpose(1, 0, 2).reshape(blocks.shape[1], -1)

    def total(blocks):
        return jnp.sum(blocks.astype(jnp.float32), axis=0)

    totals_all = jnp.sum(total(parts[6])[:6, 0].reshape(2, 3), axis=1)
    squares = totals_all * square_scale / (model_width * hidden) + STAT_EPSILON
    shrink_scale = square_scale / squares[0]
    expand_scale = square_scale / squares[1]
    shrink_newleft = 0.5 * shrink_left + unfold(parts[0]).astype(jnp.float32) * (
        0.5 * shrink_scale / model_width
    )
    shrink_newright_t = 0.5 * shrink_right.T + total(parts[3]) * (0.5 * shrink_scale / hidden)
    expand_newright_t = 0.5 * expand_right.T + unfold(parts[1]).astype(jnp.float32) * (
        0.5 * expand_scale / model_width
    )
    expand_newleft = 0.5 * expand_left + total(parts[4]) * (0.5 * expand_scale / hidden)
    expand_rows = unfold(parts[5]).astype(jnp.float32) * grad_scale
    expand_direction_t = total(parts[2]) * (grad_scale * lax.rsqrt(squares[1]))
    shrink_direction_t = (
        total(back[:, starts[-1] + 16 :])
        .reshape(dp_count // pack, block, pack, seq_count, hidden_block)
        .transpose(1, 3, 0, 2, 4)
        .reshape(block, hidden)
    ) * (grad_scale * lax.rsqrt(squares[0]))
    expand_newmoment_t, expand_newweight_t = finish(
        expand_direction_t, expand_moment.T, expand_t, model_width
    )
    shrink_newmoment_t, shrink_newweight_t = finish(
        shrink_direction_t, shrink_moment.T, shrink_t, hidden
    )
    shrink_grad = shrink_own.reshape(hidden_block, model_width) * grad_scale

    attend_newleft = 0.5 * attend_left + returned[:, 0].transpose(1, 0, 2)
    attend_newright_t = 0.5 * attend_right.transpose(1, 2, 0) + returned[:, 1]
    attend_rows = returned[:, 3].transpose(1, 0, 2) * grad_scale
    attend_newmoment_t, attend_newweight_t = finish(
        returned[:, 2], attend_moment.transpose(1, 2, 0), attend_t, model_width
    )
    return (
        layer_output,
        characters_grad,
        attend_rows,
        attend_newmoment_t.transpose(2, 0, 1),
        attend_newweight_t.transpose(2, 0, 1),
        attend_newleft,
        attend_newright_t.transpose(2, 0, 1),
        expand_rows,
        expand_newmoment_t.T,
        expand_newweight_t.T,
        expand_newleft,
        expand_newright_t.T,
        shrink_grad,
        shrink_newmoment_t.T,
        shrink_newweight_t.T,
        shrink_newleft,
        shrink_newright_t.T,
        vector_grad,
        vector_newacc,
        vector_new,
    )


def solution(mesh):
    return jax.shard_map(
        shards,
        mesh=mesh,
        in_specs=(
            P("dp", "seq", None),
            P("dp", "seq", None),
            P("dp"),
            P(),
            P(),
            P(None, None, ("seq", "dp")),
            P(None, None, ("seq", "dp")),
            P(("seq", "dp"), None, None),
            P(None, None, ("seq", "dp")),
            P(("seq", "dp"), None, None),
            P(None, None, ("seq", "dp")),
            P(None, ("seq", "dp")),
            P(None, ("seq", "dp")),
            P(("seq", "dp"), None),
            P(None, ("seq", "dp")),
            P(("seq", "dp"), None),
            P(None, ("seq", "dp")),
            P(None, ("seq", "dp")),
            P(None, ("seq", "dp")),
            P(("seq", "dp"), None),
            P(None, ("seq", "dp")),
            P(("seq", "dp"), None),
            P(None, ("seq", "dp")),
        ),
        out_specs=(
            P("dp", "seq", None),
            P("dp", "seq", None),
            P(("seq", "dp"), None, None),
            P(None, None, ("seq", "dp")),
            P(None, None, ("seq", "dp")),
            P(("seq", "dp"), None, None),
            P(None, None, ("seq", "dp")),
            P(("seq", "dp"), None),
            P(None, ("seq", "dp")),
            P(None, ("seq", "dp")),
            P(("seq", "dp"), None),
            P(None, ("seq", "dp")),
            P(("seq", "dp"), None),
            P(None, ("seq", "dp")),
            P(None, ("seq", "dp")),
            P(("seq", "dp"), None),
            P(None, ("seq", "dp")),
            P(),
            P(),
            P(),
        ),
        check_vma=False,
    )
```

```python
import functools
import math

import jax
import jax.numpy as jnp
from jax import lax
from jax.experimental import pallas as pl
from jax.experimental.pallas import tpu as pltpu
from jax.sharding import PartitionSpec as P

HEAD = 64
WIN = 128
PAIR = 2 * HEAD
KEYS = 3 * WIN
VMEM_BYTES = 56 * 1024 * 1024

EPSILON = 1e-05
STAT_EPSILON = 1e-06
MATRIX_RATE = 0.5
VECTOR_RATE = 0.3
MOMENTUM = 0.9
MASKED = -1e30

PHI_POLY = (
    0.7978849414608439,
    0.03633308457157131,
    -3.259497261642231e-05,
    -5.530619510506789e-05,
    3.964744703196676e-06,
    -1.3226336477723372e-07,
    1.7561715138424972e-09,
)


def nt(left_rows, right_rows):
    return lax.dot_general(
        left_rows, right_rows, (((1,), (1,)), ((), ())), preferred_element_type=jnp.float32
    )


def nn(left_rows, right_cols):
    return jnp.dot(left_rows, right_cols, preferred_element_type=jnp.float32)


def across(left_rows, right_rows):
    return lax.dot_general(
        left_rows, right_rows, (((0,), (0,)), ((), ())), preferred_element_type=jnp.float32
    )


def low(values):
    return values.astype(jnp.bfloat16)


def normalize(values, gain_row, bias_row):
    centre = values - jnp.mean(values, axis=-1, keepdims=True)
    spread = jnp.mean(centre * centre, axis=-1, keepdims=True)
    return centre * lax.rsqrt(spread + EPSILON) * gain_row + bias_row


def params():
    return pltpu.CompilerParams(vmem_limit_bytes=VMEM_BYTES)


def write_mask(bias_ref, length, base, blocks):
    for i in range(blocks):
        key = lax.broadcasted_iota(jnp.int32, (KEYS, WIN), 0)
        query = lax.broadcasted_iota(jnp.int32, (KEYS, WIN), 1)
        place = key + (base + (i - 1) * WIN)
        near = (key >= query) & (key <= query + 2 * WIN)
        seen = ((place >= 0) & (place < length)) | (key == query + WIN)
        bias_ref[i] = jnp.where(near & seen, 0.0, MASKED)


def stacked(rows, scale):
    lane = lax.broadcasted_iota(jnp.int32, rows.shape, 1)
    rows = rows.astype(jnp.float32) * scale
    first = jnp.where(lane < HEAD, rows, 0.0)
    second = jnp.where(lane < HEAD, 0.0, rows)
    return low(jnp.concatenate([first, second], axis=0))


def unstacked(turned):
    pair = jnp.concatenate([turned[:HEAD, :WIN], turned[HEAD:, WIN:]], axis=0)
    return pair.T


def attend_forward(blocks, lengths, base, q_ref, k_ref, v_ref, o_ref, total_ref, bias_ref):
    text = pl.program_id(0)

    @pl.when(pl.program_id(1) == 0)
    def _():
        write_mask(bias_ref, lengths[text], base[0], blocks)

    def window(ref, i):
        return ref[0, i * WIN : i * WIN + KEYS, :]

    def own(i):
        return slice(i * WIN, (i + 1) * WIN)

    every = range(blocks)
    scores = [nt(window(k_ref, i), stacked(q_ref[0, own(i), :], 0.125)) for i in every]
    weights = []
    totals = []
    for i in every:
        bias = bias_ref[i]
        masked = scores[i] + jnp.concatenate([bias, bias], axis=1)
        peak = jnp.max(masked, axis=0, keepdims=True)
        weight = jnp.exp(masked - peak)
        total = jnp.sum(weight, axis=0, keepdims=True)
        weights.append(low(weight))
        totals.append(1.0 / total)
        log_total = peak + jnp.log(total)
        total_ref[0, 0, 2 * i : 2 * i + 1, :] = log_total[:, :WIN]
        total_ref[0, 0, 2 * i + 1 : 2 * i + 2, :] = log_total[:, WIN:]
    mixed = [across(window(v_ref, i), weights[i]) for i in every]
    for i in every:
        o_ref[0, own(i), :] = low(unstacked(mixed[i] * totals[i]))


def attend_backward(
    blocks,
    extra,
    lengths,
    base,
    q_ref,
    k_ref,
    v_ref,
    up_ref,
    total_ref,
    *rest,
):
    dq_ref, dk_ref, dv_ref, bias_ref, dk_sum, dv_sum = rest[extra:]
    text = pl.program_id(0)

    @pl.when(pl.program_id(1) == 0)
    def _():
        write_mask(bias_ref, lengths[text], base[0], blocks)

    def window(i):
        return slice(i * WIN, i * WIN + KEYS)

    def own(i):
        return slice(i * WIN, (i + 1) * WIN)

    every = range(blocks)
    queries = [stacked(q_ref[0, own(i), :], 0.125) for i in every]
    upstream = [stacked(up_ref[0, own(i), :], 1.0) for i in every]
    scores = [nt(k_ref[0, window(i), :], queries[i]) for i in every]
    weight_grads = [nt(v_ref[0, window(i), :], upstream[i]) for i in every]
    weights = []
    score_grads = []
    for i in every:
        bias = bias_ref[i]
        log_total = jnp.concatenate(
            [total_ref[0, 0, 2 * i : 2 * i + 1, :], total_ref[0, 0, 2 * i + 1 : 2 * i + 2, :]],
            axis=1,
        )
        weight = jnp.exp(scores[i] + jnp.concatenate([bias, bias], axis=1) - log_total)
        product = weight * weight_grads[i]
        score_grads.append(
            low(product - weight * jnp.sum(product, axis=0, keepdims=True))
        )
        weights.append(low(weight))
    dk_sum[...] = jnp.zeros_like(dk_sum)
    dv_sum[...] = jnp.zeros_like(dv_sum)
    for i in every:
        dv_sum[window(i), :] += nn(weights[i], upstream[i])
        dk_sum[window(i), :] += nn(score_grads[i], queries[i])
    turned = [across(k_ref[0, window(i), :], score_grads[i]) for i in every]
    for i in every:
        dq_ref[0, own(i), :] = low(unstacked(turned[i]) * 0.125)
    dk_ref[0] = low(dk_sum[...])
    dv_ref[0] = low(dv_sum[...])


def attention_specs(block_size):
    wide = block_size + 2 * WIN
    blocks = block_size // WIN
    own = pl.BlockSpec((1, block_size, PAIR), lambda t, g: (t, 0, g))
    ext = pl.BlockSpec((1, wide, PAIR), lambda t, g: (t, 0, g))
    sums = pl.BlockSpec((1, 1, 2 * blocks, WIN), lambda t, g: (t, g, 0, 0))
    smem = pl.BlockSpec(memory_space=pltpu.SMEM)
    return wide, blocks, own, ext, sums, smem


def run_forward(lengths, base, query, key_ext, value_ext):
    texts, block_size, width = query.shape
    wide, blocks, own, ext, sums, smem = attention_specs(block_size)
    work = texts * blocks * (width // PAIR)
    return pl.pallas_call(
        functools.partial(attend_forward, blocks),
        grid=(texts, width // PAIR),
        in_specs=[smem, smem, own, ext, ext],
        out_specs=[own, sums],
        out_shape=[
            jax.ShapeDtypeStruct(query.shape, jnp.bfloat16),
            jax.ShapeDtypeStruct((texts, width // PAIR, 2 * blocks, WIN), jnp.float32),
        ],
        scratch_shapes=[pltpu.VMEM((blocks, KEYS, WIN), jnp.float32)],
        compiler_params=params(),
        cost_estimate=pl.CostEstimate(
            flops=work * 4 * KEYS * PAIR * 2 * WIN,
            bytes_accessed=query.size * 2 * 5,
            transcendentals=work * KEYS * 2 * WIN,
        ),
        name="attend_forward",
    )(lengths, base, query, key_ext, value_ext)


def run_backward(pairs, lengths, base, query, key_ext, value_ext, upstream, totals, kept, first):
    texts, block_size, width = query.shape
    wide = block_size + 2 * WIN
    blocks = block_size // WIN
    low_pair, count = pairs
    own = pl.BlockSpec((1, block_size, PAIR), lambda t, g: (t, 0, low_pair + g))
    ext = pl.BlockSpec((1, wide, PAIR), lambda t, g: (t, 0, low_pair + g))
    sums = pl.BlockSpec((1, 1, 2 * blocks, WIN), lambda t, g: (t, low_pair + g, 0, 0))
    smem = pl.BlockSpec(memory_space=pltpu.SMEM)
    others = tuple(kept) + tuple(first)
    work = texts * blocks * count
    return pl.pallas_call(
        functools.partial(attend_backward, blocks, len(others)),
        grid=(texts, count),
        in_specs=[smem, smem, own, ext, ext, own, sums]
        + [pl.BlockSpec(memory_space=pl.ANY)] * len(others),
        out_specs=[own, ext, ext],
        out_shape=[
            jax.ShapeDtypeStruct(query.shape, jnp.bfloat16),
            jax.ShapeDtypeStruct(key_ext.shape, jnp.bfloat16),
            jax.ShapeDtypeStruct(key_ext.shape, jnp.bfloat16),
        ],
        scratch_shapes=[
            pltpu.VMEM((blocks, KEYS, WIN), jnp.float32),
            pltpu.VMEM((wide, PAIR), jnp.float32),
            pltpu.VMEM((wide, PAIR), jnp.float32),
        ],
        input_output_aliases={7 + i: i for i in range(len(kept))},
        compiler_params=params(),
        cost_estimate=pl.CostEstimate(
            flops=work * 10 * KEYS * PAIR * 2 * WIN,
            bytes_accessed=query.size * 10,
            transcendentals=work * KEYS * 2 * WIN,
        ),
        name="attend_backward",
    )(lengths, base, query, key_ext, value_ext, upstream, totals, *others)


GATE_ROWS = 512
GATE_COLS = 256
GATE_SLAB = 32
BELL = 1.0 / math.sqrt(2.0 * math.pi)


def gate_kernel(
    rows_ref,
    upstream_ref,
    in_ref,
    out_ref,
    bias_ref,
    gate_ref,
    grad_ref,
    sums_ref,
    forward_ref,
    back_ref,
    forward_sum,
    back_sum,
):
    panel, tile = pl.program_id(0), pl.program_id(1)
    part = rows_ref.shape[1]
    ones = jnp.ones((8, GATE_ROWS), jnp.bfloat16)
    chunks = part // GATE_COLS

    def products(c):
        cols = slice(c * GATE_COLS, (c + 1) * GATE_COLS)
        hidden = nt(rows_ref[...], in_ref[cols, :]) + bias_ref[:, cols]
        return hidden, nn(upstream_ref[...], out_ref[:, cols])

    later = products(0)
    for c in range(chunks):
        hidden, hidden_grad = later
        if c + 1 < chunks:
            later = products(c + 1)
        cols = slice(c * GATE_COLS, (c + 1) * GATE_COLS)
        for i in range(GATE_ROWS // GATE_SLAB):
            own = slice(i * GATE_SLAB, (i + 1) * GATE_SLAB)
            u = hidden[own, :]
            square = u * u
            poly = PHI_POLY[-1] * square + PHI_POLY[-2]
            for term in PHI_POLY[-3::-1]:
                poly = poly * square + term
            half = 0.5 * jnp.tanh(poly * u)
            phi = half + 0.5
            bell = jnp.exp2(square * (-0.5 * math.log2(math.e)))
            gate_ref[own, cols] = low(u * phi)
            grad_ref[own, cols] = low(hidden_grad[own, :] * (phi + (u * BELL) * bell))
        sums_ref[0, :, cols] = nn(ones, grad_ref[:, cols])
    slot = pl.ds(pl.multiple_of(tile * GATE_ROWS, GATE_ROWS), GATE_ROWS)
    forward = nt(gate_ref[...], out_ref[...])
    back = nn(grad_ref[...], in_ref[...])

    @pl.when(panel == 0)
    def _():
        forward_sum[slot, :] = forward
        back_sum[slot, :] = back

    @pl.when(panel > 0)
    def _():
        forward_sum[slot, :] += forward
        back_sum[slot, :] += back

    @pl.when(panel == pl.num_programs(0) - 1)
    def _():
        forward_ref[...] = forward_sum[slot, :]
        back_ref[...] = back_sum[slot, :]


def run_gate(rows, upstream, packed, bias):
    tokens, width = rows.shape
    hidden = bias.shape[1]
    groups = hidden // width
    tiles = tokens // GATE_ROWS
    row_spec = pl.BlockSpec((GATE_ROWS, width), lambda j, i: (i, 0))
    out_spec = pl.BlockSpec((GATE_ROWS, width), lambda j, i: (i, j))
    last_spec = pl.BlockSpec(
        (GATE_ROWS, width), lambda j, i: (jnp.where(j == groups - 1, i, 0), 0)
    )
    wide_out = jax.ShapeDtypeStruct((tokens, hidden), jnp.bfloat16)
    row_out = jax.ShapeDtypeStruct((tokens, width), jnp.float32)
    return pl.pallas_call(
        gate_kernel,
        grid=(groups, tiles),
        in_specs=[
            row_spec,
            row_spec,
            pl.BlockSpec((width, width), lambda j, i: (0, 1 + groups + j)),
            pl.BlockSpec((width, width), lambda j, i: (0, 1 + j)),
            pl.BlockSpec((1, width), lambda j, i: (0, j)),
        ],
        out_specs=[
            out_spec,
            out_spec,
            pl.BlockSpec((1, 8, width), lambda j, i: (i, 0, j)),
            last_spec,
            last_spec,
        ],
        out_shape=[
            wide_out,
            wide_out,
            jax.ShapeDtypeStruct((tiles, 8, hidden), jnp.float32),
            row_out,
            row_out,
        ],
        scratch_shapes=[pltpu.VMEM((tokens, width), jnp.float32)] * 2,
        compiler_params=params(),
        cost_estimate=pl.CostEstimate(
            flops=tokens * width * hidden,
            bytes_accessed=4 * (tokens * width + width * hidden + tokens * hidden),
            transcendentals=2 * tokens * hidden,
        ),
        name="gate",
    )(rows, upstream, packed, packed, bias)


def flip(blocks, axis, mask):
    count = lax.axis_size(axis)
    return lax.ppermute(blocks, axis, [(i, i ^ mask) for i in range(count)])


def swap(blocks):
    return lax.all_to_all(blocks, "seq", split_axis=0, concat_axis=0, tiled=True)


def spread(block, axis="dp"):
    copies = jnp.broadcast_to(block[None], (lax.axis_size(axis),) + block.shape)
    return lax.all_to_all(copies, axis, split_axis=0, concat_axis=0, tiled=True)


def ordered(bit, own, other, dim):
    return jnp.where(
        bit == 0, jnp.stack([own, other], axis=dim), jnp.stack([other, own], axis=dim)
    )


def add_low(left, right):
    return low(left.astype(jnp.float32) + right.astype(jnp.float32))


def copy_kernel(value_ref, *rest):
    rest[-1][...] = value_ref[...]


def behind(value, *first):
    rows = value.reshape(-1, value.shape[-1])
    vmem = pl.BlockSpec(memory_space=pltpu.VMEM)
    return pl.pallas_call(
        copy_kernel,
        in_specs=[vmem] + [pl.BlockSpec(memory_space=pl.ANY)] * len(first),
        out_specs=vmem,
        out_shape=jax.ShapeDtypeStruct(rows.shape, rows.dtype),
        compiler_params=params(),
        name="behind",
    )(rows, *first).reshape(value.shape)


def dp_bits():
    return lax.axis_size("dp").bit_length() - 1


class Halving:
    def __init__(self, blocks, dims):
        self.blocks, self.dims = blocks, list(dims)

    def start(self, dim):
        place = self.dims.index(dim)
        axis, shift = ("seq", "cx".index(dim)) if isinstance(dim, str) else ("dp", dim)
        bit = lax.axis_index(axis) // (1 << shift) % 2
        sent = lax.dynamic_index_in_dim(self.blocks, 1 - bit, place, keepdims=False)
        self.kept = lax.dynamic_index_in_dim(self.blocks, bit, place, keepdims=False)
        self.got = flip(sent, axis, 1 << shift)
        self.dims.pop(place)

    def finish(self, last=False):
        total = self.kept.astype(jnp.float32) + self.got.astype(jnp.float32)
        self.blocks = total if last else low(total)


def rounds():
    bits = list(range(dp_bits()))
    return list(zip(["x"] + bits, bits + ["x"]))


def one_round(one, other, i, ready=()):
    left, right = rounds()[i]
    last = i == len(rounds()) - 1
    one.start(left)
    other.start(right)
    if ready:
        one.got = behind(one.got, *ready)
    one.finish(last)
    other.finish(last)
    return [mark(one.blocks), mark(other.blocks)]


def mark(array):
    return array.reshape(-1, array.shape[-1])[:8, :128]


def picker(count, block, dp_count, dp_index, width):
    row = lax.broadcasted_iota(jnp.int32, (count * block, width), 0)
    col = lax.broadcasted_iota(jnp.int32, (count * block, width), 1)
    found = jnp.zeros(row.shape, jnp.float32)
    for s in range(count):
        here = (row >= s * block) & (row < (s + 1) * block)
        place = row + (s * (dp_count - 1) + dp_index) * block
        found = jnp.where(here & (col == place), 1.0, found)
    return low(found)


def padded(rows):
    extra = -rows.shape[0] % 16
    if extra:
        rows = jnp.concatenate([rows, jnp.zeros((extra, rows.shape[1]), jnp.float32)])
    return low(rows)


def hidden_products(
    seq_count, block, dp_count, dp_index, panels, row_sets, expand_rc, expand_lw, shrink_lr, shrink_rt
):
    shrink, expand = panels[0], panels[1]
    width = shrink.shape[0]
    pick = picker(seq_count, block, dp_count, dp_index, width)
    shrink_cols = low(nt(pick, shrink))
    expand_cols = nt(pick, expand)
    turned = low(nt(shrink_rt, low(nn(shrink_lr, shrink))))
    shrink_right = nn(shrink_cols, shrink)
    expand_left = nn(low(expand_cols), expand)
    expand_turned = nt(low(nn(expand_rc, expand)), expand_lw)
    owned = expand_rc.shape[0] // seq_count
    sums = [
        jnp.sum(jnp.sum(jnp.square(p.astype(jnp.float32)), axis=0, keepdims=True), axis=1, keepdims=True)
        for p in (shrink, expand)
    ]
    line = lax.broadcasted_iota(jnp.int32, (16, width), 0)
    marks = jnp.zeros((16, width), jnp.float32)
    for i, value in enumerate(sums):
        for j in range(3):
            piece = low(jnp.broadcast_to(value, (16, width))).astype(jnp.float32)
            marks = jnp.where(line == 3 * i + j, piece, marks)
            value = value - piece[:1, :1]
    pieces = []
    for s in range(seq_count):
        rows = slice(s * owned, (s + 1) * owned)
        few = slice(s * block, (s + 1) * block)
        pieces.append(
            [
                padded(nt(row_sets[s, 0], shrink)),
                padded(nt(row_sets[s, 1], expand)),
                padded(expand_turned[rows]),
                padded(shrink_right[few]),
                padded(expand_left[few]),
                padded(expand_cols[few]),
                low(marks),
            ]
        )
    return pieces, turned


def hidden_kernel(
    seq_count,
    block,
    dp_count,
    index_ref,
    panels_ref,
    rows_ref,
    expand_rc_ref,
    expand_lw_ref,
    shrink_lr_ref,
    shrink_rt_ref,
    token_ref,
    out_ref,
    turn_ref,
):
    pieces, turned = hidden_products(
        seq_count,
        block,
        dp_count,
        index_ref[0],
        panels_ref,
        rows_ref,
        expand_rc_ref[...],
        expand_lw_ref[...],
        shrink_lr_ref[...],
        shrink_rt_ref[...],
    )
    turn_ref[...] = turned
    for s in range(seq_count):
        start = 0
        for piece in pieces[s]:
            out_ref[s, start : start + piece.shape[0], :] = piece
            start += piece.shape[0]


def run_hidden(seq_count, block, dp_count, dp_index, panels, row_sets, rc, lw, lr, rt, token):
    width = panels.shape[1]
    owned = rc.shape[0] // seq_count
    if owned % 16 or block % 8:
        pieces, turned = hidden_products(
            seq_count, block, dp_count, dp_index, panels, row_sets, rc, lw, lr, rt
        )
        return jnp.stack([jnp.concatenate(piece) for piece in pieces]), turned
    few = block + -block % 16
    rows_out = 3 * owned + 3 * few + 16
    vmem = pl.BlockSpec(memory_space=pltpu.VMEM)
    return pl.pallas_call(
        functools.partial(hidden_kernel, seq_count, block, dp_count),
        in_specs=[pl.BlockSpec(memory_space=pltpu.SMEM)]
        + [vmem] * 6
        + [pl.BlockSpec(memory_space=pl.ANY)],
        out_specs=[vmem, vmem],
        out_shape=[
            jax.ShapeDtypeStruct((seq_count, rows_out, width), jnp.bfloat16),
            jax.ShapeDtypeStruct((width, seq_count * owned), jnp.bfloat16),
        ],
        compiler_params=params(),
        cost_estimate=pl.CostEstimate(
            flops=40 * owned * width * width, bytes_accessed=12 * width * width, transcendentals=0
        ),
        name="hidden_update",
    )(dp_index.reshape(1), panels, row_sets, rc, lw, lr, rt, token)


def halves_of(values, keep=lambda high: high):
    extra = 16 - values.shape[0]
    if extra:
        values = jnp.concatenate([values, jnp.zeros((extra, values.shape[1]), jnp.float32)])
    high = keep(low(values))
    return jnp.concatenate([high, low(values - high.astype(jnp.float32))])


def from_halves(parts):
    total = jnp.sum(parts.astype(jnp.float32), axis=0)
    return total[:16] + total[16:]


def attend_products(seq_count, block, dp_count, dp_index, scale, whole, own, rc, lw):
    width = whole.shape[0]
    pick = picker(seq_count, block, dp_count, dp_index, width)
    wide = whole.astype(jnp.float32)
    total = jnp.sum(jnp.sum(wide * wide, axis=0, keepdims=True), axis=1, keepdims=True)
    square = total * (scale * scale / (width * width)) + STAT_EPSILON
    gram = (0.5 * scale * scale / width) / square
    left = nt(low(own), whole) * gram
    right = nn(low(nt(pick, whole)), whole) * gram
    turned = nt(low(nt(rc, whole)), lw) * (scale * lax.rsqrt(square))
    return [
        [padded(piece[s * block : (s + 1) * block]) for piece in (left, right, turned, own)]
        for s in range(seq_count)
    ]


def attend_kernel(
    seq_count,
    block,
    dp_count,
    scale,
    index_ref,
    whole_ref,
    own_ref,
    rc_ref,
    lw_ref,
    vector_ref,
    token_ref,
    out_ref,
):
    vectors = halves_of(from_halves(vector_ref[...]))
    pieces = attend_products(
        seq_count,
        block,
        dp_count,
        index_ref[0],
        scale,
        whole_ref[...],
        own_ref[...],
        rc_ref[...],
        lw_ref[...],
    )
    for s in range(seq_count):
        for i, piece in enumerate(pieces[s]):
            out_ref[s, i] = piece
        out_ref[s, len(pieces[s])] = vectors


def run_attend(seq_count, block, dp_count, dp_index, scale, whole, own, rc, lw, vectors, token):
    width = whole.shape[0]
    few = block + -block % 16
    if few != 32 or block % 8:
        pieces = attend_products(
            seq_count, block, dp_count, dp_index, scale, whole, own, rc, lw
        )
        sums = halves_of(from_halves(vectors), lax.optimization_barrier)
        fill = ((0, 32 - few), (0, 0))
        return jnp.stack(
            [jnp.stack([jnp.pad(p, fill) for p in piece] + [sums]) for piece in pieces]
        )
    vmem = pl.BlockSpec(memory_space=pltpu.VMEM)
    return pl.pallas_call(
        functools.partial(attend_kernel, seq_count, block, dp_count, scale),
        in_specs=[pl.BlockSpec(memory_space=pltpu.SMEM)]
        + [vmem] * 5
        + [pl.BlockSpec(memory_space=pl.ANY)],
        out_specs=vmem,
        out_shape=jax.ShapeDtypeStruct((seq_count, 5, few, width), jnp.bfloat16),
        compiler_params=params(),
        cost_estimate=pl.CostEstimate(
            flops=10 * own.shape[0] * width * width, bytes_accessed=6 * width * width, transcendentals=0
        ),
        name="attend_update",
    )(dp_index.reshape(1), whole, own, rc, lw, vectors, token)


def finish(direction, moment, weight, row_count):
    new_moment = MOMENTUM * moment + direction
    new_weight = weight - MATRIX_RATE / math.sqrt(row_count) * new_moment
    return (new_moment, new_weight)


def shards(
    characters,
    cotangent,
    lengths,
    vectors,
    vector_acc,
    attend_weight,
    attend_moment,
    attend_left,
    attend_right,
    attend_rootleft,
    attend_rootright,
    expand_weight,
    expand_moment,
    expand_left,
    expand_right,
    expand_rootleft,
    expand_rootright,
    shrink_weight,
    shrink_moment,
    shrink_left,
    shrink_right,
    shrink_rootleft,
    shrink_rootright,
):
    text_count, block_size, model_width = characters.shape
    token_rows = text_count * block_size
    both = ("seq", "dp")
    seq_count = lax.axis_size("seq")
    dp_count = lax.axis_size("dp")
    seq_index = lax.axis_index("seq")
    dp_index = lax.axis_index("dp")
    core = seq_index % 2
    chip = seq_index // 2
    tokens_all = token_rows * seq_count * dp_count
    grad_scale = 1.0 / math.sqrt(tokens_all)
    square_scale = grad_scale * grad_scale
    hidden = expand_weight.shape[1] * seq_count * dp_count
    part = hidden // seq_count
    block = model_width // (seq_count * dp_count)
    hidden_block = hidden // (seq_count * dp_count)
    rows_own = seq_count * block

    owners = seq_count * dp_count
    groups = hidden // model_width
    ends = seq_count - 1
    before = lax.ppermute(
        characters[:, block_size - WIN :], "seq", [(i, i + 1) for i in range(ends)]
    )
    follow = lax.ppermute(characters[:, :WIN], "seq", [(i + 1, i) for i in range(ends)])

    attend_t = attend_weight.transpose(1, 2, 0)
    expand_t = expand_weight.T
    shrink_t = shrink_weight.T
    packed = jnp.concatenate(
        [
            low(attend_t[3]),
            low(shrink_t)
            .reshape(block, owners, groups, block)
            .transpose(0, 2, 1, 3)
            .reshape(block, hidden),
            low(expand_t)
            .reshape(groups, block, model_width)
            .transpose(1, 0, 2)
            .reshape(block, hidden),
        ],
        axis=1,
    )
    packed_all = lax.all_gather(packed, both, axis=0, tiled=True)
    over_dp = spread(low(attend_t[:3])).transpose(1, 0, 2, 3)

    def panels_of(rows):
        return low(rows).reshape(rows.shape[0], seq_count, part).transpose(1, 0, 2)

    def copies_of(rows):
        return jnp.broadcast_to(low(rows)[None], (seq_count,) + rows.shape)

    root_parts = jnp.concatenate(
        [
            panels_of(expand_rootright.T),
            low(attend_rootright.transpose(1, 2, 0)),
            panels_of(shrink_rootleft),
            low(attend_rootleft).transpose(1, 0, 2),
            copies_of(expand_rootleft),
            copies_of(shrink_rootright.T),
        ],
        axis=1,
    )
    over_chip = ordered(chip, over_dp, flip(over_dp, "seq", 2), 1)

    input_ext = jnp.concatenate([before, characters, follow], axis=1)
    wide = block_size + 2 * WIN

    gain_one = vectors[0]
    bias_one = vectors[1]
    query_bias = vectors[2]
    value_bias = vectors[3]
    out_bias = vectors[4]
    gain_two = vectors[5]
    bias_two = vectors[6]
    shrink_bias = vectors[7]
    expand_bias = vectors[8:].reshape(owners, groups, block).transpose(1, 0, 2).reshape(1, -1)
    normed_ext = low(normalize(input_ext.astype(jnp.float32), gain_one, bias_one))
    over_core = ordered(core, over_chip, flip(over_chip, "seq", 1), 2)
    qkv_t = over_core.reshape(3 * model_width, model_width)
    normed_low = normed_ext[:, WIN : WIN + block_size].reshape(token_rows, model_width)
    ext_rows = normed_ext.reshape(text_count * wide, model_width)
    query_low = low(nt(normed_low, qkv_t[:model_width]) + query_bias).reshape(characters.shape)
    key_ext = low(nt(ext_rows, qkv_t[model_width : 2 * model_width])).reshape(
        text_count, wide, model_width
    )
    value_ext = low(nt(ext_rows, qkv_t[2 * model_width :]) + value_bias).reshape(
        text_count, wide, model_width
    )
    base = (seq_index * block_size).astype(jnp.int32).reshape(1)
    attended, totals = run_forward(lengths, base, query_low, key_ext, value_ext)
    roots = swap(behind(root_parts, attended))
    attended_low = attended.reshape(token_rows, model_width)

    out_t = packed_all[:, :model_width]
    layer_input = characters.astype(jnp.float32).reshape(token_rows, model_width)
    middle = layer_input + nt(attended_low, out_t) + out_bias
    normed_two_low = low(normalize(middle, gain_two, bias_two))
    cut = 2 * hidden_block + block
    upstream = cotangent.reshape(token_rows, model_width)
    gated_low, expanded_grad, expand_sums, forward, normed_two_grad = run_gate(
        normed_two_low, upstream, packed_all, expand_bias
    )
    layer_output = low(middle + forward + shrink_bias).reshape(characters.shape)

    bits = dp_bits()
    grid_dims = (2,) * (2 + bits)
    link_dims = ["x", "c"] + list(range(bits - 1, -1, -1))

    def hidden_sum(left_rows, right_rows):
        sums = low(across(left_rows, right_rows))
        return Halving(
            sums.reshape((groups,) + grid_dims + (block, model_width)), [None] + link_dims
        )

    shrink_sum = hidden_sum(gated_low, upstream)
    shrink_sum.start("c")
    expand_sum = hidden_sum(expanded_grad, normed_two_low)
    expand_sum.start("c")
    shrink_sum.finish()
    expand_sum.finish()
    marks = [mark(shrink_sum.blocks), mark(expand_sum.blocks)]

    upstream_float = upstream.astype(jnp.float32)
    grad_shrink_bias = jnp.sum(upstream_float, axis=0)
    grad_expand_bias = (
        jnp.sum(expand_sums[:, 0], axis=0)
        .reshape(groups, owners, block)
        .transpose(1, 0, 2)
        .reshape(groups, model_width)
    )

    unused_norm, norm_two_back = jax.vjp(normalize, middle, gain_two, bias_two)
    middle_part, grad_gain_two, grad_bias_two = norm_two_back(normed_two_grad)
    middle_grad = upstream_float + middle_part
    branch_grad = low(middle_grad)
    grad_out_bias = jnp.sum(branch_grad.astype(jnp.float32), axis=0)
    grad_out = low(across(attended_low, branch_grad))
    attended_grad = low(nn(branch_grad, out_t)).reshape(characters.shape)
    pairs = model_width // PAIR
    early = 2 * pairs // 3
    kept = run_backward(
        (0, early), lengths, base, query_low, key_ext, value_ext, attended_grad, totals, (), marks
    )
    marks = one_round(shrink_sum, expand_sum, 0)
    root_all = lax.all_gather(behind(roots[:, cut:], *marks), "dp", axis=1)
    kept = run_backward(
        (early, pairs - early),
        lengths,
        base,
        query_low,
        key_ext,
        value_ext,
        attended_grad,
        totals,
        kept,
        marks,
    )
    query_grad, key_grad, value_grad = kept
    one_round(shrink_sum, expand_sum, 1)

    pair_grad = jnp.stack([key_grad, value_grad])
    from_above = lax.ppermute(
        pair_grad[:, :, :WIN], "seq", [(i + 1, i) for i in range(ends)]
    )
    from_below = lax.ppermute(
        pair_grad[:, :, block_size + WIN :], "seq", [(i, i + 1) for i in range(ends)]
    )
    pair_own = pair_grad[:, :, WIN : WIN + block_size]
    pair_low = jnp.concatenate(
        [
            add_low(pair_own[:, :, :WIN], from_below),
            pair_own[:, :, WIN : block_size - WIN],
            add_low(pair_own[:, :, block_size - WIN :], from_above),
        ],
        axis=2,
    ).reshape(2, token_rows, model_width)
    query_rows = query_grad.reshape(token_rows, model_width)
    grads = jnp.stack(
        [
            low(across(normed_low, query_rows)),
            low(across(normed_low, pair_low[0])),
            low(across(normed_low, pair_low[1])),
            grad_out,
        ]
    ).reshape((2, 2) + (2, seq_count // 2) + (2,) * bits + (block, model_width))
    core_sum = Halving(grads, ["x", "c"])
    core_sum.start("c")
    core_sum.finish()
    for i in range(2, len(rounds())):
        one_round(shrink_sum, expand_sum, i)
    shrink_own, expand_own = shrink_sum.blocks, expand_sum.blocks
    hidden_own = jnp.stack(
        [low(own).reshape(hidden_block, model_width) for own in (shrink_own, expand_own)]
    )

    halves = [
        Halving(core_sum.blocks[:, i], ["x", None] + list(range(bits - 1, -1, -1)))
        for i in range(2)
    ]
    expand_rc = roots[:, :hidden_block].reshape(seq_count * hidden_block, part)
    attend_rc = roots[:, hidden_block : hidden_block + block].reshape(rows_own, model_width)
    shrink_lr = roots[:, hidden_block + block : cut].reshape(seq_count * hidden_block, part)
    attend_lw = root_all[:, :, :block].reshape(model_width, model_width)
    expand_lw = root_all[:, :, block : 2 * block].reshape(model_width, model_width)
    shrink_rt = root_all[:, :, 2 * block :].transpose(1, 0, 2, 3).reshape(model_width, model_width)

    panels = lax.all_gather(hidden_own, "dp", axis=1, tiled=True)
    row_sets = ordered(chip, hidden_own, flip(hidden_own, "seq", 2), 0)
    row_sets = ordered(core, row_sets, flip(row_sets, "seq", 1), 1)
    row_sets = row_sets.reshape((seq_count,) + hidden_own.shape)
    ready = (row_sets, expand_rc, expand_lw, shrink_lr, shrink_rt, attend_rc, attend_lw)
    for i in range(len(rounds())):
        one_round(*halves, i, ready=ready if i == len(rounds()) - 1 else ())
    attend_own = jnp.concatenate([half.blocks for half in halves])
    grad_query_bias = jnp.sum(query_rows.astype(jnp.float32), axis=0)
    grad_value_bias = jnp.sum(pair_low[1].astype(jnp.float32), axis=0)
    normed_grad = (
        nn(query_rows, qkv_t[:model_width])
        + nn(pair_low[0], qkv_t[model_width : 2 * model_width])
        + nn(pair_low[1], qkv_t[2 * model_width :])
    )
    unused_first, norm_one_back = jax.vjp(normalize, layer_input, gain_one, bias_one)
    input_part, grad_gain_one, grad_bias_one = norm_one_back(normed_grad)
    characters_grad = low(middle_grad + input_part).reshape(characters.shape)
    vector_terms = jnp.concatenate(
        [
            jnp.stack(
                [
                    grad_gain_one,
                    grad_bias_one,
                    grad_query_bias,
                    grad_value_bias,
                    grad_out_bias,
                    grad_gain_two,
                    grad_bias_two,
                    grad_shrink_bias,
                ]
            ),
            grad_expand_bias.reshape(-1, model_width),
        ],
        axis=0,
    )
    token = attend_own[0, :1, :128] + attend_own[-1, :1, :128]
    attend_all = lax.all_gather(
        jnp.concatenate(
            [
                low(attend_own).reshape(rows_own, model_width),
                halves_of(vector_terms, lax.optimization_barrier),
            ]
        ),
        "dp",
        axis=0,
    )
    whole = (
        attend_all[:, :rows_own]
        .reshape(dp_count, seq_count, block, model_width)
        .transpose(1, 0, 2, 3)
        .reshape(model_width, model_width)
    )

    index = dp_index.astype(jnp.int32)
    products, turned = run_hidden(
        seq_count,
        block,
        dp_count,
        index,
        panels,
        row_sets,
        expand_rc,
        expand_lw,
        shrink_lr,
        shrink_rt,
        token,
    )
    turned = lax.all_to_all(
        turned.reshape(dp_count, rows_own, seq_count * hidden_block),
        "dp",
        split_axis=0,
        concat_axis=0,
        tiled=True,
    )
    pack = model_width // (seq_count * hidden_block)
    turned = (
        turned.reshape(dp_count // pack, pack, seq_count, block, seq_count * hidden_block)
        .transpose(2, 0, 3, 1, 4)
        .reshape(seq_count, hidden_block, model_width)
    )
    to_owners = jnp.concatenate([products, turned], axis=1)
    back = swap(to_owners)
    to_return = run_attend(
        seq_count,
        block,
        dp_count,
        index,
        grad_scale,
        whole,
        attend_own.reshape(rows_own, model_width),
        attend_rc,
        attend_lw,
        attend_all[:, rows_own:],
        mark(back),
    )
    returned = swap(to_return)
    vector_sum = from_halves(returned[:, 4])[: vectors.shape[0]]
    returned = returned[:, :4, :block].astype(jnp.float32)
    vector_grad = vector_sum * grad_scale
    vector_newacc = vector_acc + vector_grad * vector_grad
    vector_new = vectors - VECTOR_RATE * vector_grad / (jnp.sqrt(vector_newacc) + 1e-08)

    few = block + -block % 16
    much = hidden_block + -hidden_block % 16
    starts = [0, much, 2 * much, 3 * much, 3 * much + few, 3 * much + 2 * few, 3 * much + 3 * few]
    sizes = [hidden_block] * 3 + [block] * 3 + [16]
    parts = [back[:, i : i + n] for i, n in zip(starts, sizes)]

    def unfold(blocks):
        return blocks.transpose(1, 0, 2).reshape(blocks.shape[1], -1)

    def total(blocks):
        return jnp.sum(blocks.astype(jnp.float32), axis=0)

    totals_all = jnp.sum(total(parts[6])[:6, 0].reshape(2, 3), axis=1)
    squares = totals_all * square_scale / (model_width * hidden) + STAT_EPSILON
    shrink_scale = square_scale / squares[0]
    expand_scale = square_scale / squares[1]
    shrink_newleft = 0.5 * shrink_left + unfold(parts[0]).astype(jnp.float32) * (
        0.5 * shrink_scale / model_width
    )
    shrink_newright_t = 0.5 * shrink_right.T + total(parts[3]) * (0.5 * shrink_scale / hidden)
    expand_newright_t = 0.5 * expand_right.T + unfold(parts[1]).astype(jnp.float32) * (
        0.5 * expand_scale / model_width
    )
    expand_newleft = 0.5 * expand_left + total(parts[4]) * (0.5 * expand_scale / hidden)
    expand_rows = unfold(parts[5]).astype(jnp.float32) * grad_scale
    expand_direction_t = total(parts[2]) * (grad_scale * lax.rsqrt(squares[1]))
    shrink_direction_t = (
        total(back[:, starts[-1] + 16 :])
        .reshape(dp_count // pack, block, pack, seq_count, hidden_block)
        .transpose(1, 3, 0, 2, 4)
        .reshape(block, hidden)
    ) * (grad_scale * lax.rsqrt(squares[0]))
    expand_newmoment_t, expand_newweight_t = finish(
        expand_direction_t, expand_moment.T, expand_t, model_width
    )
    shrink_newmoment_t, shrink_newweight_t = finish(
        shrink_direction_t, shrink_moment.T, shrink_t, hidden
    )
    shrink_grad = shrink_own.reshape(hidden_block, model_width) * grad_scale

    attend_newleft = 0.5 * attend_left + returned[:, 0].transpose(1, 0, 2)
    attend_newright_t = 0.5 * attend_right.transpose(1, 2, 0) + returned[:, 1]
    attend_rows = returned[:, 3].transpose(1, 0, 2) * grad_scale
    attend_newmoment_t, attend_newweight_t = finish(
        returned[:, 2], attend_moment.transpose(1, 2, 0), attend_t, model_width
    )
    return (
        layer_output,
        characters_grad,
        attend_rows,
        attend_newmoment_t.transpose(2, 0, 1),
        attend_newweight_t.transpose(2, 0, 1),
        attend_newleft,
        attend_newright_t.transpose(2, 0, 1),
        expand_rows,
        expand_newmoment_t.T,
        expand_newweight_t.T,
        expand_newleft,
        expand_newright_t.T,
        shrink_grad,
        shrink_newmoment_t.T,
        shrink_newweight_t.T,
        shrink_newleft,
        shrink_newright_t.T,
        vector_grad,
        vector_newacc,
        vector_new,
    )


def solution(mesh):
    return jax.shard_map(
        shards,
        mesh=mesh,
        in_specs=(
            P("dp", "seq", None),
            P("dp", "seq", None),
            P("dp"),
            P(),
            P(),
            P(None, None, ("seq", "dp")),
            P(None, None, ("seq", "dp")),
            P(("seq", "dp"), None, None),
            P(None, None, ("seq", "dp")),
            P(("seq", "dp"), None, None),
            P(None, None, ("seq", "dp")),
            P(None, ("seq", "dp")),
            P(None, ("seq", "dp")),
            P(("seq", "dp"), None),
            P(None, ("seq", "dp")),
            P(("seq", "dp"), None),
            P(None, ("seq", "dp")),
            P(None, ("seq", "dp")),
            P(None, ("seq", "dp")),
            P(("seq", "dp"), None),
            P(None, ("seq", "dp")),
            P(("seq", "dp"), None),
            P(None, ("seq", "dp")),
        ),
        out_specs=(
            P("dp", "seq", None),
            P("dp", "seq", None),
            P(("seq", "dp"), None, None),
            P(None, None, ("seq", "dp")),
            P(None, None, ("seq", "dp")),
            P(("seq", "dp"), None, None),
            P(None, None, ("seq", "dp")),
            P(("seq", "dp"), None),
            P(None, ("seq", "dp")),
            P(None, ("seq", "dp")),
            P(("seq", "dp"), None),
            P(None, ("seq", "dp")),
            P(("seq", "dp"), None),
            P(None, ("seq", "dp")),
            P(None, ("seq", "dp")),
            P(("seq", "dp"), None),
            P(None, ("seq", "dp")),
            P(),
            P(),
            P(),
        ),
        check_vma=False,
    )
```
